32 devices in a mesh: parts: 2 (over x), tp: 16 (over z, y, core).
Axes of the slice: x: 2, y: 2, z: 4, core: 2. Of those that a mesh axis runs over, the one named last changes fastest.
Arguments:
- x_in: bfloat16 [64, 4, 5120], P('parts', None, 'tp'), parts along dimension 0, may hold values from -6 to 6
- ln_gain: bfloat16 [5120], P('tp'), may hold values from 0.5 to 1.5
- w_query: bfloat16 [5120, 8192], P(None, 'tp'), may hold values from -0.078125 to 0.078125
- w_key: bfloat16 [5120, 1024], P(None, 'tp'), may hold values from -0.078125 to 0.078125
- w_value: bfloat16 [5120, 1024], P(None, 'tp'), may hold values from -0.078125 to 0.078125
- w_out: bfloat16 [8192, 5120], P('tp'), may hold values from -0.0625 to 0.0625
- q_gain: bfloat16 [128], replicated, may hold values from 0.5 to 1.5
- k_gain: bfloat16 [128], replicated, may hold values from 0.5 to 1.5
- a_query: bfloat16 [5120, 64], P('tp'), may hold values from -0.078125 to 0.078125
- a_key: bfloat16 [5120, 64], P('tp'), may hold values from -0.078125 to 0.078125
- a_value: bfloat16 [5120, 64], P('tp'), may hold values from -0.078125 to 0.078125
- b_query: bfloat16 [64, 8192], P(None, 'tp'), may hold values from -0.75 to 0.75
- b_key: bfloat16 [64, 1024], P(None, 'tp'), may hold values from -0.75 to 0.75
- b_value: bfloat16 [64, 1024], P(None, 'tp'), may hold values from -0.75 to 0.75
- a_out: bfloat16 [8192, 64], P('tp'), may hold values from -0.0625 to 0.0625
- b_out: bfloat16 [64, 5120], P(None, 'tp'), may hold values from -0.75 to 0.75
- key_cache: bfloat16 [64, 1024, 1024], P(('parts', 'tp')), parts along dimension 0, may hold values from -2.5 to 2.5
- value_cache: bfloat16 [64, 1024, 1024], P(('parts', 'tp')), parts along dimension 0, may hold values from -2.5 to 2.5
- kv_length: int32 [64], P(('parts', 'tp')), parts along dimension 0, may hold values from 1 to 1024, as said below
- cand_rows: bfloat16 [64, 8, 5120], P(('parts', 'tp')), parts along dimension 0, may hold values from -0.078125 to 0.078125
- final_gain: bfloat16 [5120], replicated, may hold values from 0.099609375 to 1.8984375
- row_owner: int32 [64, 1], P('parts'), parts along dimension 0, may hold values from 0 to 15; in each aligned block of 32 rows (0 to 31, 32 to 63, ...) at most 4 rows name the same one
Outputs:
- hidden_out: bfloat16 [64, 4, 5120], P(('parts', 'tp')), parts along dimension 0
- cand_logprob: float32 [128, 32], P(('parts', 'tp')), parts along dimension 0
The draws below stay inside these ranges and needn't reach their ends.
There are 2 independent parts, one for each index of `parts`. The reference program is written for one: setup_inputs(seed, part) draws one part's arguments, and reference() takes and returns one part's arrays. A program takes and returns all parts, laid end to end along the dimension named above; an argument that names none is the same for every part. Nothing has to cross between parts.
Inputs may be any that keep to these rules, and one draw needn't show every extreme that they name: `kv_length`: one row holds exactly 1024 cached positions and another exactly 1. `row_owner`: no tp index owns more than 4 rows, some owns exactly 4, and every index owns at least one.
All inputs are finite; a program needn't handle non-finite values.
Results may differ from the reference program's by a relative error of at most 0.007.
Values may be sent and summed in bfloat16 or wider, within the bound.
A program may use at most 128 MiB of HBM per device.

```python
import math
import jax
import jax.numpy as jnp
import numpy as np
from jax import lax

D = 5120
H = 64
KVH = 8
HD = 128
RANK = 64
SPAN = 1024
STEPS = 4
CANDS = 8
ROWS = 32
CAP = 4
N_TP = 16


def draw_kv_length(key, part):
    key = jax.random.fold_in(key, 11)
    first_key, second_key = jax.random.split(key)
    base_lengths = jax.random.randint(first_key, (ROWS,), 1, SPAN + 1, dtype=jnp.int32)
    shuffled = jax.random.permutation(second_key, ROWS)
    position = jnp.arange(ROWS, dtype=jnp.int32)
    lengths = jnp.where(position == shuffled[0], SPAN, base_lengths)
    return jnp.where(position == shuffled[1], 1, lengths).astype(jnp.int32)


def block_scale(own_key, extent, cuts, least, largest):
    gain = 1.0
    for dim, parts in cuts:
        draws = jax.random.uniform(jax.random.fold_in(jax.random.fold_in(own_key, 6), dim), (parts,), jnp.float32, least / len(cuts), largest / len(cuts))
        gain = gain * jnp.repeat(jnp.exp(draws), extent[dim] // parts).reshape((-1,) + (1,) * (len(extent) - 1 - dim))
    return gain


def routed_block(own_key, own, number, rows, amount, top, most, slope):
    sequence = jax.random.permutation(own_key, amount)
    packed, common = shares(amount, rows * top, most, slope, True), shares(amount, rows * top, most, slope, False)
    places = jnp.arange(amount)

    def named(sizes, offset_by):
        used = int((sizes > 0).sum())
        fixed = max(1, used // 4)
        shifted = fixed + (places - fixed + offset_by * (used - fixed)) % max(1, amount - fixed)
        return jnp.zeros((amount,), jnp.int32).at[sequence[jnp.where(places < fixed, places, shifted)]].set(jnp.asarray(sizes, jnp.int32))

    sizes = jnp.where(number % 4 == 0, named(packed, number // 4), named(common, number - number // 4 - 1))
    mixed = jax.random.permutation(jax.random.fold_in(own, 3), amount)
    donor, receiver = mixed[0:amount // 2 * 2:2], mixed[1:amount // 2 * 2:2]
    slack = jnp.minimum(sizes[donor] - 1, most - sizes[receiver]) // 2
    slack = jnp.where((donor == sequence[0]) | (receiver == sequence[0]) | (sizes[receiver] == 0), 0, jnp.maximum(slack, 0))
    shifted = jax.random.randint(jax.random.fold_in(own, 4), (amount // 2,), 0, 1 << 20) % (slack + 1)
    sizes = sizes.at[donor].add(-shifted).at[receiver].add(shifted)
    items = jnp.searchsorted(jnp.cumsum(sizes), jnp.arange(rows * top), side="right").astype(jnp.int32)
    grid = items.reshape(top, rows).T
    grid = grid[jax.random.permutation(jax.random.fold_in(own, 1), rows)]
    offset_by = jax.random.randint(jax.random.fold_in(own, 2), (rows, 1), 0, top)
    return jnp.take_along_axis(grid, (jnp.arange(top)[None, :] + offset_by) % top, axis=1)


def shares(count, total, limit, lean, full):
    portions = [(1 << 20) // math.isqrt(grade ** lean) + 1 for grade in range(1, count + 1)]
    largest = limit if full else min(limit, max(-(-total // count), total * portions[0] // sum(portions)))
    least = 1 if total - largest >= count - 1 else 0
    given, spare = [largest] + [least] * (count - 1), total - largest - least * (count - 1)
    while spare > 0:
        movable = [i for i in range(1, count) if given[i] < largest] or [i for i in range(1, count) if given[i] < limit]
        pool, budget = sum([portions[i] for i in movable]), spare
        for i in movable:
            more = min(limit - given[i], max(1, budget * portions[i] // pool), spare)
            given[i] = given[i] + more
            spare = spare - more
    return np.array(given)


def normal_values(stream_key, dims, scale, limit, pieces=(), held_as=jnp.bfloat16):
    factor_of = block_scale(stream_key, dims, pieces, -0.22, 0.18) if pieces else 1.0
    array = jax.random.normal(stream_key, dims, jnp.float32) * scale * factor_of
    return jnp.minimum(jnp.maximum(array, -limit), limit).astype(held_as)


def setup_inputs(seed: int = 0, part: int = 0) -> dict:
    splits = jax.random.split(jax.random.key(seed), 23)
    own_keys = jax.random.split(jax.random.fold_in(splits[22], part), 23)
    x_in = normal_values(own_keys[0], (ROWS, STEPS, D), 1.0, 6.0, ((2, 16),))
    ln_gain = jnp.clip(1.0 + 0.1 * jax.random.normal(splits[1], (D,), jnp.float32), 0.5, 1.5).astype(jnp.bfloat16)
    w_query = normal_values(splits[2], (D, H * HD), D ** -0.5, 0.078125, ((1, 16),))
    w_key = normal_values(splits[3], (D, KVH * HD), D ** -0.5, 0.078125, ((1, 16),))
    w_value = normal_values(splits[4], (D, KVH * HD), D ** -0.5, 0.078125, ((1, 16),))
    w_out = normal_values(splits[5], (H * HD, D), (H * HD) ** -0.5, 0.0625, ((0, 16),))
    q_gain = jnp.clip(1.0 + 0.1 * jax.random.normal(splits[6], (HD,), jnp.float32), 0.5, 1.5).astype(jnp.bfloat16)
    k_gain = jnp.clip(1.0 + 0.1 * jax.random.normal(splits[7], (HD,), jnp.float32), 0.5, 1.5).astype(jnp.bfloat16)
    a_query = normal_values(splits[8], (D, RANK), D ** -0.5, 0.078125, ((0, 16),))
    a_key = normal_values(splits[9], (D, RANK), D ** -0.5, 0.078125, ((0, 16),))
    a_value = normal_values(splits[10], (D, RANK), D ** -0.5, 0.078125, ((0, 16),))
    b_query = normal_values(splits[11], (RANK, H * HD), RANK ** -0.5, 0.75, ((1, 16),))
    b_key = normal_values(splits[12], (RANK, KVH * HD), RANK ** -0.5, 0.75, ((1, 16),))
    b_value = normal_values(splits[13], (RANK, KVH * HD), RANK ** -0.5, 0.75, ((1, 16),))
    a_out = normal_values(splits[14], (H * HD, RANK), (H * HD) ** -0.5, 0.0625, ((0, 16),))
    b_out = normal_values(splits[15], (RANK, D), RANK ** -0.5, 0.75, ((1, 16),))
    key_cache = normal_values(own_keys[16], (ROWS, SPAN, KVH * HD), 1.0, 2.5, ((0, 16),))
    value_cache = normal_values(own_keys[17], (ROWS, SPAN, KVH * HD), 1.0, 2.5, ((0, 16),))
    kv_length = draw_kv_length(jax.random.fold_in(jax.random.fold_in(splits[22], part), 71), part)
    cand_rows = normal_values(own_keys[19], (ROWS, CANDS, D), D ** -0.5, 0.078125, ((0, 16),))
    final_gain = jnp.clip(1.0 + 0.18 * jax.random.normal(splits[20], (D,), jnp.float32), 0.099609375, 1.8984375).astype(jnp.bfloat16)
    row_owner_keys = jax.random.split(jax.random.fold_in(own_keys[21], 1), ROWS // ROWS)
    row_owner_turns = jax.random.permutation(jax.random.fold_in(own_keys[21], 3), ROWS // ROWS)
    row_owner = jax.vmap(lambda own, number: routed_block(jax.random.fold_in(own_keys[21], 2), own, number, ROWS, N_TP, 1, CAP, 2))(row_owner_keys, row_owner_turns).reshape((ROWS, 1))
    return {"x_in": x_in, "ln_gain": ln_gain, "w_query": w_query, "w_key": w_key, "w_value": w_value, "w_out": w_out, "q_gain": q_gain, "k_gain": k_gain, "a_query": a_query, "a_key": a_key, "a_value": a_value, "b_query": b_query, "b_key": b_key, "b_value": b_value, "a_out": a_out, "b_out": b_out, "key_cache": key_cache, "value_cache": value_cache, "kv_length": kv_length, "cand_rows": cand_rows, "final_gain": final_gain, "row_owner": row_owner}


EPSILON = 1e-06
ROPE_BASE = 1000000.0

def scale_of(values):
    return lax.rsqrt(lax.optimization_barrier(jnp.mean(values * values, axis=-1, keepdims=True)) + EPSILON)

def rotary(values, position):
    half_size = values.shape[-1] // 2
    frequency = ROPE_BASE ** (-jnp.arange(half_size, dtype=jnp.float32) / half_size)
    angles = position.astype(jnp.float32)[:, :, None, None] * frequency
    angles = jnp.concatenate([angles, angles], axis=-1)
    turned = jnp.concatenate([-values[..., half_size:], values[..., :half_size]], axis=-1)
    return values * jnp.cos(angles) + turned * jnp.sin(angles)

def head_norm(values, gain_vec, position):
    floated = values.astype(jnp.float32)
    return rotary(floated * scale_of(floated) * gain_vec.astype(jnp.float32), position).astype(jnp.bfloat16)

def live_mask(lengths, span_len, step_count):
    column = jnp.arange(span_len + step_count, dtype=jnp.int32)[None, None, :]
    step_ids = jnp.arange(step_count, dtype=jnp.int32)[None, :, None]
    cached = (column < lengths[:, None, None]) & (column < span_len)
    fresh = (column >= span_len) & (column - span_len <= step_ids)
    return (cached | fresh).astype(jnp.float32)

def slot_of(row_owner, shards, capacity):
    owned_rows = (row_owner[:, None] == jnp.arange(shards, dtype=jnp.int32)[None, :]).astype(jnp.int32)
    before = jnp.cumsum(owned_rows, axis=0) - owned_rows
    return row_owner * capacity + lax.optimization_barrier(jnp.sum(before * owned_rows, axis=1))

def project(normed, weight, down_factor, up_factor):
    base_part = jnp.dot(normed, weight, preferred_element_type=jnp.float32)
    low_part = jnp.dot(normed, down_factor, preferred_element_type=jnp.float32)
    return base_part + jnp.dot(low_part, up_factor.astype(jnp.float32), precision=lax.Precision.HIGHEST)

def attend(queries, new_keys, new_values, key_cache, value_cache, lengths):
    row_count, step_count, head_count, head_size = queries.shape
    group_count = new_keys.shape[2]
    span_len = key_cache.shape[1]
    key_all = jnp.concatenate([key_cache, new_keys.reshape(row_count, step_count, group_count * head_size)], axis=1)
    value_all = jnp.concatenate([value_cache, new_values], axis=1)
    key_all = key_all.reshape(row_count, span_len + step_count, group_count, head_size).astype(jnp.float32)
    value_all = value_all.reshape(row_count, span_len + step_count, group_count, head_size).astype(jnp.float32)
    grouped = queries.reshape(row_count, step_count, group_count, head_count // group_count, head_size).astype(jnp.float32)
    scores = jnp.einsum('rsngd,rtnd->rsngt', grouped, key_all) / math.sqrt(head_size)
    weights = jnp.exp(scores) * live_mask(lengths, span_len, step_count)[:, :, None, None, :]
    weights = (weights / lax.optimization_barrier(jnp.sum(weights, axis=-1, keepdims=True))).astype(jnp.bfloat16)
    mixed_heads = jnp.einsum('rsngt,rtnd->rsngd', weights.astype(jnp.float32), value_all)
    return mixed_heads.reshape(row_count, step_count, head_count * head_size).astype(jnp.bfloat16)

def reference(x_in, ln_gain, w_query, w_key, w_value, w_out, q_gain, k_gain, a_query, a_key, a_value, b_query, b_key, b_value, a_out, b_out, key_cache, value_cache, kv_length, cand_rows, final_gain, row_owner):
    row_count, step_count, full_width = x_in.shape
    x_float = x_in.astype(jnp.float32)
    normed = (x_float * scale_of(x_float) * ln_gain.astype(jnp.float32)).astype(jnp.bfloat16)
    flat_normed = normed.reshape(row_count * step_count, full_width)
    query_lin = project(flat_normed, w_query, a_query, b_query).astype(jnp.bfloat16)
    key_lin = project(flat_normed, w_key, a_key, b_key).astype(jnp.bfloat16)
    value_lin = project(flat_normed, w_value, a_value, b_value).astype(jnp.bfloat16)
    position = kv_length[:, None] + jnp.arange(step_count, dtype=jnp.int32)[None, :]
    queries = head_norm(query_lin.reshape(row_count, step_count, H, HD), q_gain, position)
    new_keys = head_norm(key_lin.reshape(row_count, step_count, KVH, HD), k_gain, position)
    new_values = value_lin.reshape(row_count, step_count, KVH * HD)

    def one_row(members):
        return attend(*[member[None] for member in members])[0]
    attended = lax.map(one_row, (queries, new_keys, new_values, key_cache, value_cache, kv_length))
    flat_attended = attended.reshape(row_count * step_count, H * HD)
    mixed_out = project(flat_attended, w_out, a_out, b_out).reshape(row_count, step_count, full_width)
    hidden_out = (x_float + mixed_out).astype(jnp.bfloat16)
    hidden_float = hidden_out.astype(jnp.float32)
    final_normed = (hidden_float * scale_of(hidden_float) * final_gain.astype(jnp.float32)).astype(jnp.bfloat16)
    logits = jnp.einsum('rsd,rkd->rsk', final_normed.astype(jnp.float32), cand_rows.astype(jnp.float32))
    logprob = logits - jnp.log(lax.optimization_barrier(jnp.sum(jnp.exp(logits), axis=-1, keepdims=True)))
    slot_index = slot_of(row_owner[:, 0], N_TP, CAP)
    placing = (slot_index[:, None] == jnp.arange(N_TP * CAP, dtype=jnp.int32)[None, :]).astype(jnp.float32)
    cand_logprob = jnp.dot(placing.T, logprob.reshape(row_count, step_count * CANDS), precision=lax.Precision.HIGHEST)
    return (hidden_out, cand_logprob)
```

```python
import math

import jax
import jax.numpy as jnp
import numpy as np
from jax import lax
from jax.experimental import pallas as pl
from jax.experimental.pallas import tpu as pltpu
from jax.sharding import PartitionSpec as P

CAP = 4


EPSILON = 1e-06
ROPE_BASE = 1000000.0


def scale_of(values):
    return lax.rsqrt(jnp.mean(values * values, axis=-1, keepdims=True) + EPSILON)


def rotary(values, position):
    half_size = values.shape[-1] // 2
    frequency = ROPE_BASE ** (-jnp.arange(half_size, dtype=jnp.float32) / half_size)
    angles = position.astype(jnp.float32)[:, :, None, None] * frequency
    angles = jnp.concatenate([angles, angles], axis=-1)
    turned = jnp.concatenate([-values[..., half_size:], values[..., :half_size]], axis=-1)
    return values * jnp.cos(angles) + turned * jnp.sin(angles)


def head_norm(values, gain_vec, position):
    floated = values.astype(jnp.float32)
    return rotary(floated * scale_of(floated) * gain_vec.astype(jnp.float32), position).astype(
        jnp.bfloat16
    )


def live_mask(lengths, span_len, step_count):
    column = jnp.arange(span_len + step_count, dtype=jnp.int32)[None, None, :]
    step_ids = jnp.arange(step_count, dtype=jnp.int32)[None, :, None]
    cached = (column < lengths[:, None, None]) & (column < span_len)
    fresh = (column >= span_len) & (column - span_len <= step_ids)
    return (cached | fresh).astype(jnp.float32)


def slot_of(row_owner, shards, capacity):
    owned_rows = (row_owner[:, None] == jnp.arange(shards, dtype=jnp.int32)[None, :]).astype(
        jnp.int32
    )
    before = jnp.cumsum(owned_rows, axis=0) - owned_rows
    return row_owner * capacity + jnp.sum(before * owned_rows, axis=1)


def exact_dot(left, right):
    return jnp.dot(left, right.astype(jnp.float32), precision=lax.Precision.HIGHEST)


def attend(queries, new_keys, new_values, key_cache, value_cache, lengths):
    row_count, step_count, head_count, head_size = queries.shape
    group_count = new_keys.shape[2]
    span_len = key_cache.shape[1]
    key_all = jnp.concatenate(
        [key_cache, new_keys.reshape(row_count, step_count, group_count * head_size)], axis=1
    )
    value_all = jnp.concatenate([value_cache, new_values], axis=1)
    key_all = key_all.reshape(row_count, span_len + step_count, group_count, head_size)
    value_all = value_all.reshape(row_count, span_len + step_count, group_count, head_size)
    grouped = queries.reshape(
        row_count, step_count, group_count, head_count // group_count, head_size
    )
    scores = jnp.einsum(
        "rsngd,rtnd->rsngt", grouped, key_all, preferred_element_type=jnp.float32
    ) / math.sqrt(head_size)
    weights = jnp.exp(scores) * live_mask(lengths, span_len, step_count)[:, :, None, None, :]
    weights = (weights / jnp.sum(weights, axis=-1, keepdims=True)).astype(jnp.bfloat16)
    mixed_heads = jnp.einsum(
        "rsngt,rtnd->rsngd", weights, value_all, preferred_element_type=jnp.float32
    )
    return mixed_heads.reshape(row_count, step_count, head_count * head_size).astype(jnp.bfloat16)


def on_device(
    x_in,
    ln_gain,
    w_query,
    w_key,
    w_value,
    w_out,
    q_gain,
    k_gain,
    a_query,
    a_key,
    a_value,
    b_query,
    b_key,
    b_value,
    a_out,
    b_out,
    key_cache,
    value_cache,
    kv_length,
    cand_rows,
    final_gain,
    row_owner,
):
    shards = lax.axis_size("tp")
    device_index = lax.axis_index("tp")
    row_count, step_count, part_width = x_in.shape
    full_width = part_width * shards
    local_rows = row_count // shards
    head_size = q_gain.shape[0]
    head_cols = w_query.shape[1]
    kv_cols = w_key.shape[1]
    rank_size = a_query.shape[1]
    x_float = x_in.astype(jnp.float32)
    squares = lax.psum(jnp.sum(x_float * x_float, axis=-1), "tp")
    inverse = lax.rsqrt(squares / full_width + EPSILON)[..., None]
    normed = (x_float * inverse * ln_gain.astype(jnp.float32)).astype(jnp.bfloat16)
    flat_normed = normed.reshape(row_count * step_count, part_width)
    base_weight = jnp.concatenate([w_query, w_key, w_value], axis=1)
    partial_low = jnp.concatenate(
        [
            jnp.dot(flat_normed, a_query, preferred_element_type=jnp.float32),
            jnp.dot(flat_normed, a_key, preferred_element_type=jnp.float32),
            jnp.dot(flat_normed, a_value, preferred_element_type=jnp.float32),
        ],
        axis=1,
    )
    low_full = lax.psum(partial_low, "tp")
    weight_parts = (base_weight,)
    lifted = jnp.concatenate(
        [
            exact_dot(low_full[:, :rank_size], b_query),
            exact_dot(low_full[:, rank_size : 2 * rank_size], b_key),
            exact_dot(low_full[:, 2 * rank_size :], b_value),
        ],
        axis=1,
    )
    part_weight = weight_parts[0]
    running = jnp.dot(
        lax.all_gather(flat_normed, "tp", axis=1, tiled=True),
        part_weight,
        preferred_element_type=jnp.float32,
    )
    projected = running + lifted
    mixed_proj = projected.astype(jnp.bfloat16).reshape(
        row_count, step_count, head_cols + 2 * kv_cols
    )
    by_row = lax.all_to_all(mixed_proj, "tp", split_axis=0, concat_axis=2, tiled=True)
    by_row = by_row.reshape(local_rows, step_count, shards, head_cols + 2 * kv_cols)
    query_lin = by_row[..., :head_cols].reshape(local_rows, step_count, -1, head_size)
    key_lin = by_row[..., head_cols : head_cols + kv_cols].reshape(
        local_rows, step_count, -1, head_size
    )
    value_lin = by_row[..., head_cols + kv_cols :].reshape(local_rows, step_count, shards * kv_cols)
    position = kv_length[:, None] + jnp.arange(step_count, dtype=jnp.int32)[None, :]
    queries = head_norm(query_lin, q_gain, position)
    new_keys = head_norm(key_lin, k_gain, position)
    attended = attend(queries, new_keys, value_lin, key_cache, value_cache, kv_length)
    by_head = lax.all_to_all(attended, "tp", split_axis=2, concat_axis=0, tiled=True)
    up_full = lax.all_gather(b_out, "tp", axis=1, tiled=True)
    segment = by_head.reshape(lax.axis_size("tp") * local_rows * step_count, head_cols)
    summed = lax.psum_scatter(
        (
            jnp.dot(segment, w_out, preferred_element_type=jnp.float32)
            + exact_dot(jnp.dot(segment, a_out, preferred_element_type=jnp.float32), up_full)
        ).reshape(lax.axis_size("tp") * local_rows, step_count, full_width),
        "tp",
        scatter_dimension=0,
        tiled=True,
    )
    residual = lax.all_to_all(x_in, "tp", split_axis=0, concat_axis=2, tiled=True)
    hidden_out = (residual.astype(jnp.float32) + summed).astype(jnp.bfloat16)
    hidden_float = hidden_out.astype(jnp.float32)
    final_normed = (hidden_float * scale_of(hidden_float) * final_gain.astype(jnp.float32)).astype(
        jnp.bfloat16
    )
    logits = jnp.einsum("rsd,rkd->rsk", final_normed, cand_rows, preferred_element_type=jnp.float32)
    logprob = logits - jnp.log(jnp.sum(jnp.exp(logits), axis=-1, keepdims=True))
    logprob = logprob.reshape(local_rows, step_count * cand_rows.shape[1])
    slot_index = slot_of(row_owner[:, 0], shards, CAP)
    all_rows = lax.all_gather(logprob, "tp", axis=0, tiled=True)
    wanted = device_index * CAP + jnp.arange(CAP, dtype=jnp.int32)
    select = (slot_index[None, :] == wanted[:, None]).astype(jnp.float32)
    cand_logprob = jnp.dot(select, all_rows, precision=lax.Precision.HIGHEST)
    return (hidden_out, cand_logprob)


MESH = pl.DeviceIdType.MESH
NZ, NY, NC = 4, 2, 2
FUSED_TP = NZ * NY * NC
CHUNKS = 4
F32, BF16 = jnp.float32, jnp.bfloat16


def dot_nt(left, right):
    return lax.dot_general(left, right, (((1,), (1,)), ((), ())), preferred_element_type=F32)


def dot_nn(left, right):
    return jnp.dot(left, right, preferred_element_type=F32)


def split_high_low(values):
    high = values.astype(BF16)
    return high, (values - high.astype(F32)).astype(BF16)


def fused_kernel(
    x_ref, gain_ref, wq_hbm, wk_hbm, wv_hbm, wo_hbm, qg_ref, kg_ref, aq_ref, ak_ref, av_ref,
    bq_ref, bk_ref, bv_ref, ao_ref, bo_ref, kc_hbm, vc_hbm, len_ref, cand_ref, fg_ref, freq_ref,
    pick_ref,
    hid_ref, lp_ref,
    wq, wkv, wo, keys, vals, xall, ball, lowp, lowr, lowall, upm, accq, acckv, xres, bfull,
    projs, projr, atts, attr, parts, got_c, half_y, got_y, quarter, got_z, hidden, lpall,
    local_sem, xs, xr, bs, br, l1s, l1r, l2s, l2r, ps, pr, ats, atr,
    cs, cr, ys, yr, zs, zr, gs, gr,
):
    n = FUSED_TP
    me = lax.axis_index("tp")
    core, y, z = lax.rem(me, NC), lax.rem(me // NC, NY), me // (NC * NY)
    groups, rows8, part = x_ref.shape
    width = part * n
    rank = aq_ref.shape[0]
    span = kc_hbm.shape[1]
    padded = keys.shape[1]
    head = qg_ref.shape[1]
    qcols = wq.shape[1]
    rows = groups * rows8
    chunk = width // CHUNKS

    def place(pz, py, pc):
        return (pz * NY + py) * NC + pc

    y_peer, c_peer = place(z, 1 - y, core), place(z, y, 1 - core)

    def remote(source, target, send, recv, device):
        return pltpu.make_async_remote_copy(
            src_ref=source, dst_ref=target, send_sem=send, recv_sem=recv,
            device_id={"tp": device}, device_id_type=MESH,
        )

    loads = [
        pltpu.make_async_copy(wq_hbm, wq, local_sem.at[0]),
        pltpu.make_async_copy(wk_hbm, wkv.at[pl.ds(0, wk_hbm.shape[0])], local_sem.at[1]),
        pltpu.make_async_copy(wv_hbm, wkv.at[pl.ds(wk_hbm.shape[0], wk_hbm.shape[0])], local_sem.at[2]),
        pltpu.make_async_copy(kc_hbm.at[0], keys.at[0, pl.ds(0, span)], local_sem.at[3]),
        pltpu.make_async_copy(kc_hbm.at[1], keys.at[1, pl.ds(0, span)], local_sem.at[4]),
        pltpu.make_async_copy(vc_hbm.at[0], vals.at[0, pl.ds(0, span)], local_sem.at[5]),
        pltpu.make_async_copy(vc_hbm.at[1], vals.at[1, pl.ds(0, span)], local_sem.at[6]),
        pltpu.make_async_copy(wo_hbm, wo, local_sem.at[7]),
    ]
    for load in loads:
        load.start()

    barrier = pltpu.get_barrier_semaphore()

    def greet(d, carry):
        pl.semaphore_signal(barrier, inc=1, device_id={"tp": lax.rem(me + d, n)}, device_id_type=MESH)
        return carry

    lax.fori_loop(1, n, greet, 0)

    xall[me, 0:groups] = x_ref[...]
    xall[me, groups] = jnp.broadcast_to(gain_ref[...].astype(F32), (rows8, part)).astype(BF16)
    ball[me] = bo_ref[...]
    pl.semaphore_wait(barrier, n - 1)

    def gather(buffer, send, recv):
        def hop(block, device, number):
            return remote(buffer.at[block], buffer.at[block], send.at[number], recv.at[block], device)

        def begin():
            hop(me, y_peer, 0).start()
            for dz in range(1, NZ):
                hop(me, place(lax.rem(z + dz, NZ), y, core), dz).start()
            hop(me, c_peer, NZ).start()

        def middle():
            for dz in range(1, NZ):
                block = place(lax.rem(z + dz, NZ), y, core)
                hop(block, y_peer, 0).wait_recv()
                hop(block, y_peer, NZ + dz).start()
                hop(block, c_peer, 2 * NZ - 1 + dz).start()

        def late():
            for dz in range(NZ):
                block = place(lax.rem(z + dz, NZ), 1 - y, core)
                hop(block, c_peer, 0).wait_recv()
                hop(block, c_peer, 3 * NZ - 1 + dz).start()

        def finish():
            for dz in range(NZ):
                for py in range(NY):
                    hop(place(lax.rem(z + dz, NZ), py, 1 - core), c_peer, 0).wait_recv()

        def drain():
            for number in range(n - 1):
                hop(me, c_peer, number).wait_send()

        return begin, middle, late, finish, drain

    def exchange(source, target, send, recv, spread):
        def copy(to, slot, device):
            part_of = source.at[me] if spread else source.at[to]
            return remote(part_of, target.at[slot], send.at[to], recv.at[slot], device)

        def begin():
            def one(d, carry):
                to = lax.rem(me + d, n)
                copy(to, me, to).start()
                return carry

            lax.fori_loop(1, n, one, 0)

        def finish():
            def one(d, carry):
                other = lax.rem(me + d, n)
                copy(other, other, other).wait_recv()
                return carry

            lax.fori_loop(1, n, one, 0)

        def drain():
            def one(d, carry):
                other = lax.rem(me + d, n)
                copy(other, other, other).wait_send()
                return carry

            lax.fori_loop(1, n, one, 0)

        return begin, finish, drain

    x_gather = gather(xall, xs, xr)
    b_gather = gather(ball, bs, br)
    low_scatter = exchange(lowp, lowr, l1s, l1r, False)
    low_spread = exchange(lowall, lowall, l2s, l2r, True)
    proj_swap = exchange(projs, projr, ps, pr, False)
    att_swap = exchange(atts, attr, ats, atr, False)
    lp_spread = exchange(lpall, lpall, gs, gr, True)

    x_gather[0]()

    own = x_ref[...].astype(F32).reshape(rows, part)
    own_gained = (own * gain_ref[...].astype(F32)).astype(BF16)
    down = jnp.concatenate([aq_ref[...], ak_ref[...], av_ref[...], jnp.zeros((rank, part), BF16)], axis=0)
    low_part = dot_nt(own_gained, down)
    square = jnp.sum(own * own, axis=-1, keepdims=True)
    lane = lax.broadcasted_iota(jnp.int32, low_part.shape, 1)
    lowp[...] = jnp.where(lane < 3 * rank, low_part, square).reshape(lowp.shape)
    lowr[me] = lowp[me]
    low_scatter[0]()

    upm[...] = jnp.zeros_like(upm)
    upm[0:rank, 0:qcols] = bq_ref[...]
    empty = jnp.zeros(bk_ref.shape, F32)
    upm[rank : 2 * rank, qcols:] = jnp.concatenate([bk_ref[...].astype(F32), empty], axis=1).astype(BF16)
    upm[2 * rank : 3 * rank, qcols:] = jnp.concatenate([empty, bv_ref[...].astype(F32)], axis=1).astype(BF16)
    for r in range(2):
        keys[r, span:padded] = jnp.zeros((padded - span, keys.shape[2]), BF16)
        vals[r, span:padded] = jnp.zeros((padded - span, vals.shape[2]), BF16)
    sub8 = lax.broadcasted_iota(jnp.int32, (rows8, head), 0)
    lane8 = lax.broadcasted_iota(jnp.int32, (rows8, head), 1)
    steps = rows8 // 2
    position = jnp.where(sub8 < steps, len_ref[0] + sub8, len_ref[1] + sub8 - steps).astype(F32)
    angle = position * freq_ref[...]
    cosine = jnp.cos(angle)[None]
    sine = jnp.sin(angle)
    sine = jnp.where(lane8 < head // 2, -sine, sine)[None]

    x_gather[1]()
    low_scatter[1]()
    lowall[me] = jnp.sum(lowr[...], axis=0)
    low_spread[0]()
    x_gather[2]()
    for load in loads[:3]:
        load.wait()
    x_gather[3]()
    b_gather[0]()

    pair = NC * part
    for m in range(n // 2):
        sides, kept = [], []
        for b in (2 * m, 2 * m + 1):
            block = xall[b, 0:groups].astype(F32).reshape(rows, part)
            sides.append(block * xall[b, groups].astype(F32)[0:1])
            kept.append(xall[b, me].astype(F32))
        gained = jnp.concatenate(sides, axis=1).astype(BF16)
        xres[:, m * pair : (m + 1) * pair] = jnp.concatenate(kept, axis=1)
        more_q = dot_nn(gained, wq[m * pair : (m + 1) * pair, :])
        more_kv = dot_nt(gained, wkv[:, m * pair : (m + 1) * pair])
        accq[...] = more_q if m == 0 else accq[...] + more_q
        acckv[...] = more_kv if m == 0 else acckv[...] + more_kv

    low_spread[1]()
    low_all = lowall[...].reshape(rows, lowall.shape[2])
    inverse = lax.rsqrt(low_all[:, 3 * rank : 3 * rank + 1] / width + EPSILON)
    low_high, low_low = split_high_low(jnp.where(lane < 3 * rank, low_all * inverse, 0.0))
    lifted = dot_nn(low_high, upm[...]) + dot_nn(low_low, upm[...])
    projs[:, :, 0:qcols] = (accq[...] * inverse + lifted[:, 0:qcols]).reshape(groups, rows8, qcols).astype(BF16)
    projs[:, :, qcols:] = (acckv[...] * inverse + lifted[:, qcols:]).reshape(groups, rows8, head).astype(BF16)
    projr[me] = projs[me]
    proj_swap[0]()
    b_gather[1]()
    proj_swap[1]()
    b_gather[2]()

    def normed_heads(values, gain_row):
        scaled = values * lax.rsqrt(jnp.mean(values * values, axis=-1, keepdims=True) + EPSILON)
        scaled = scaled * gain_row[...].astype(F32)[None]
        return scaled * cosine + pltpu.roll(scaled, head // 2, 2) * sine

    sub16 = lax.broadcasted_iota(jnp.int32, (n, rows8, head), 1)
    by_row = [[], []]
    for p in range(qcols // (2 * head)):
        first = normed_heads(projr[:, :, 2 * p * head : (2 * p + 1) * head].astype(F32), qg_ref)
        second = normed_heads(projr[:, :, (2 * p + 1) * head : (2 * p + 2) * head].astype(F32), qg_ref)
        by_row[0].append(jnp.where(sub16 < steps, first, pltpu.roll(second, steps, 1)))
        by_row[1].append(jnp.where(sub16 < steps, pltpu.roll(first, steps, 1), second))
    kv_groups = n // 2
    kv_all = projr[:, :, qcols:].astype(F32).reshape(kv_groups, 2, rows8, head)
    even, odd = kv_all[:, 0], kv_all[:, 1]
    lane_kv = lax.broadcasted_iota(jnp.int32, even.shape, 2)
    new_keys = normed_heads(jnp.where(lane_kv < head // 2, even, pltpu.roll(odd, head // 2, 2)), kg_ref)
    new_vals = jnp.where(lane_kv < head // 2, pltpu.roll(even, head // 2, 2), odd)

    for load in loads[3:7]:
        load.wait()
    blank = jnp.zeros((rows8, head), F32)
    for g in range(kv_groups):
        new_key = jnp.concatenate([new_keys[g], blank], axis=0).astype(BF16)
        new_val = jnp.concatenate([new_vals[g], blank], axis=0).astype(BF16)
        for r in range(2):
            keys[r, span : span + 2 * rows8, g * head : (g + 1) * head] = new_key
            vals[r, span : span + 2 * rows8, g * head : (g + 1) * head] = new_val

    asked = 4 * rows8
    column = lax.broadcasted_iota(jnp.int32, (asked, padded), 1)
    step_of = lax.rem(lax.broadcasted_iota(jnp.int32, (asked, padded), 0), steps)
    live = []
    for r in range(2):
        fresh = column - span - r * steps
        in_cache = (column < len_ref[r]) & (column < span)
        live.append((in_cache | ((fresh >= 0) & (fresh <= step_of) & (column >= span))).astype(F32))
    sub4 = lax.broadcasted_iota(jnp.int32, (4, rows8, head), 1)
    for g in range(kv_groups):
        outs = []
        for r in range(2):
            tiles = [by_row[r][p][2 * g + side][None] for side in range(2) for p in range(2)]
            query = jnp.concatenate(tiles, axis=0).reshape(asked, head).astype(BF16)
            scores = dot_nt(query, keys[r, :, g * head : (g + 1) * head]) * (1.0 / math.sqrt(head))
            weights = jnp.exp(scores) * live[r]
            total = jnp.sum(weights, axis=-1, keepdims=True)
            mixed = dot_nn(weights.astype(BF16), vals[r, :, g * head : (g + 1) * head]) / total
            outs.append(mixed.reshape(4, rows8, head))
        first = jnp.where(sub4 < steps, outs[0], pltpu.roll(outs[1], steps, 1)).astype(BF16)
        second = jnp.where(sub4 < steps, pltpu.roll(outs[0], steps, 1), outs[1]).astype(BF16)
        for side in range(2):
            for p in range(2):
                atts[2 * g + side, :, 2 * p * head : (2 * p + 1) * head] = first[2 * side + p]
                atts[2 * g + side, :, (2 * p + 1) * head : (2 * p + 2) * head] = second[2 * side + p]
    attr[me] = atts[me]
    att_swap[0]()
    b_gather[3]()
    for m in range(n // 2):
        bfull[:, m * pair : (m + 1) * pair] = jnp.concatenate(
            [ball[2 * m].astype(F32), ball[2 * m + 1].astype(F32)], axis=1
        ).astype(BF16)
    loads[7].wait()
    att_swap[1]()

    segment = attr[...].astype(F32).reshape(rows, qcols).astype(BF16)
    inner_high, inner_low = split_high_low(dot_nt(segment, ao_ref[...]))

    def c_hop(k):
        return remote(parts.at[k, 1 - core], got_c.at[k], cs.at[k], cr.at[k], c_peer)

    def y_hop(k):
        return remote(half_y.at[k, 1 - y], got_y.at[k], ys.at[k], yr.at[k], y_peer)

    def z_hop(k, dz):
        other = lax.rem(z + dz, NZ)
        return remote(quarter.at[k, other], got_z.at[k, dz - 1], zs.at[k, dz - 1], zr.at[k, dz - 1], place(other, y, core))

    def multiply(k):
        at = slice(k * chunk, (k + 1) * chunk)
        up = bfull[:, at]
        out = dot_nn(segment, wo[:, at]) + (dot_nn(inner_high, up) + dot_nn(inner_low, up))
        out = out.reshape(groups // NC, NC, rows8, chunk).astype(BF16)
        for pc in range(NC):
            parts[k, pc] = out[:, pc]
        c_hop(k).start()

    def over_y(k):
        c_hop(k).wait_recv()
        both = parts[k, core].astype(F32) + got_c[k].astype(F32)
        both = both.reshape(NZ, NY, rows8, chunk).astype(BF16)
        for py in range(NY):
            half_y[k, py] = both[:, py]
        y_hop(k).start()

    def over_z(k):
        y_hop(k).wait_recv()
        quarter[k] = (half_y[k, y].astype(F32) + got_y[k].astype(F32)).astype(BF16)
        for dz in range(1, NZ):
            z_hop(k, dz).start()

    for k in range(CHUNKS):
        multiply(k)
        if k >= 1:
            over_y(k - 1)
    over_y(CHUNKS - 1)
    for k in range(CHUNKS):
        over_z(k)

    squares = jnp.zeros((rows8, 1), F32)
    for k in range(CHUNKS):
        at = slice(k * chunk, (k + 1) * chunk)
        total = xres[:, at] + quarter[k, z].astype(F32)
        for dz in range(1, NZ):
            z_hop(k, dz).wait_recv()
            total = total + got_z[k, dz - 1].astype(F32)
        rounded = total.astype(BF16)
        hid_ref[:, at] = rounded
        rounded = rounded.astype(F32)
        hidden[:, at] = rounded
        squares = squares + jnp.sum(rounded * rounded, axis=-1, keepdims=True)
    final = (hidden[...] * lax.rsqrt(squares / width + EPSILON) * fg_ref[...].astype(F32)).astype(BF16)
    cands = cand_ref.shape[1]
    logits = jnp.where(
        lax.broadcasted_iota(jnp.int32, (rows8, cands), 0) < steps,
        dot_nt(final, cand_ref[0]),
        dot_nt(final, cand_ref[1]),
    )
    logprob = logits - jnp.log(jnp.sum(jnp.exp(logits), axis=-1, keepdims=True))
    lpall[me] = jnp.concatenate([logprob, jnp.zeros((rows8, lpall.shape[2] - cands), F32)], axis=1)
    lp_spread[0]()
    lp_spread[1]()
    placed = jnp.dot(
        pick_ref[...], lpall[...].reshape(rows, lpall.shape[2]),
        precision=lax.Precision.HIGHEST, preferred_element_type=F32,
    )
    lp_ref[...] = placed[:, 0:cands]

    x_gather[4]()
    b_gather[4]()
    for swap in (low_scatter, low_spread, proj_swap, att_swap, lp_spread):
        swap[2]()
    for k in range(CHUNKS):
        c_hop(k).wait_send()
        y_hop(k).wait_send()
        for dz in range(1, NZ):
            z_hop(k, dz).wait_send()


def fused_on_device(
    x_in, ln_gain, w_query, w_key, w_value, w_out, q_gain, k_gain, a_query, a_key, a_value,
    b_query, b_key, b_value, a_out, b_out, key_cache, value_cache, kv_length, cand_rows,
    final_gain, row_owner,
):
    n = lax.axis_size("tp")
    me = lax.axis_index("tp")
    row_count, step_count, part = x_in.shape
    rows8 = row_count * step_count // n
    width = part * n
    head = q_gain.shape[0]
    qcols = w_query.shape[1]
    kvcols = w_key.shape[1]
    cols = qcols + 2 * kvcols
    rank = a_query.shape[1]
    span, kv_width = key_cache.shape[1:]
    cands = cand_rows.shape[1]
    half = head // 2
    frequency = ROPE_BASE ** (-np.arange(half, dtype=np.float32) / np.float32(half))
    frequency = jnp.asarray(np.concatenate([frequency, frequency])[None, :].astype(np.float32))

    slot_index = slot_of(row_owner[:, 0], n, CAP)
    wanted = me * CAP + jnp.arange(CAP, dtype=jnp.int32)
    select = (slot_index[None, :] == wanted[:, None]).astype(F32)
    same_step = jnp.eye(step_count, dtype=F32)
    pick = (select[:, None, :, None] * same_step[None, :, None, :]).reshape(
        CAP * step_count, row_count * step_count
    )

    chunk = width // CHUNKS
    rows = row_count * step_count
    padded = span + 128
    vmem = pl.BlockSpec(memory_space=pltpu.VMEM)
    smem = pl.BlockSpec(memory_space=pltpu.SMEM)
    hbm = pl.BlockSpec(memory_space=pl.ANY)
    dma = pltpu.SemaphoreType.DMA
    hidden_out, cand_logprob = pl.pallas_call(
        fused_kernel,
        out_shape=(
            jax.ShapeDtypeStruct((rows8, width), BF16),
            jax.ShapeDtypeStruct((CAP * step_count, cands), F32),
        ),
        in_specs=[vmem, vmem, hbm, hbm, hbm, hbm, vmem, vmem, vmem, vmem, vmem,
                  vmem, vmem, vmem, vmem, vmem, hbm, hbm, smem, vmem, vmem, vmem, vmem],
        out_specs=(vmem, vmem),
        scratch_shapes=[
            pltpu.VMEM((width, qcols), BF16),
            pltpu.VMEM((2 * kvcols, width), BF16),
            pltpu.VMEM((qcols, width), BF16),
            pltpu.VMEM((2, padded, kv_width), BF16),
            pltpu.VMEM((2, padded, kv_width), BF16),
            pltpu.VMEM((n, n + 1, rows8, part), BF16),
            pltpu.VMEM((n, rank, part), BF16),
            pltpu.VMEM((n, rows8, 4 * rank), F32),
            pltpu.VMEM((n, rows8, 4 * rank), F32),
            pltpu.VMEM((n, rows8, 4 * rank), F32),
            pltpu.VMEM((4 * rank, cols), BF16),
            pltpu.VMEM((rows, qcols), F32),
            pltpu.VMEM((rows, 2 * kvcols), F32),
            pltpu.VMEM((rows8, width), F32),
            pltpu.VMEM((rank, width), BF16),
            pltpu.VMEM((n, rows8, cols), BF16),
            pltpu.VMEM((n, rows8, cols), BF16),
            pltpu.VMEM((n, rows8, qcols), BF16),
            pltpu.VMEM((n, rows8, qcols), BF16),
            pltpu.VMEM((CHUNKS, NC, NZ * NY, rows8, chunk), BF16),
            pltpu.VMEM((CHUNKS, NZ * NY, rows8, chunk), BF16),
            pltpu.VMEM((CHUNKS, NY, NZ, rows8, chunk), BF16),
            pltpu.VMEM((CHUNKS, NZ, rows8, chunk), BF16),
            pltpu.VMEM((CHUNKS, NZ, rows8, chunk), BF16),
            pltpu.VMEM((CHUNKS, NZ - 1, rows8, chunk), BF16),
            pltpu.VMEM((rows8, width), F32),
            pltpu.VMEM((n, rows8, 128), F32),
            dma((8,)),
            dma((n,)), dma((n,)), dma((n,)), dma((n,)),
            dma((n,)), dma((n,)), dma((n,)), dma((n,)),
            dma((n,)), dma((n,)), dma((n,)), dma((n,)),
            dma((CHUNKS,)), dma((CHUNKS,)), dma((CHUNKS,)), dma((CHUNKS,)),
            dma((CHUNKS, NZ - 1)), dma((CHUNKS, NZ - 1)),
            dma((n,)), dma((n,)),
        ],
        compiler_params=pltpu.CompilerParams(
            collective_id=0, has_side_effects=True, vmem_limit_bytes=56 * 1024 * 1024
        ),
        name="layer",
    )(
        x_in.reshape(n, rows8, part), ln_gain[None, :], w_query, w_key.T, w_value.T, w_out,
        q_gain[None, :], k_gain[None, :], a_query.T, a_key.T, a_value.T, b_query, b_key, b_value,
        a_out.T, b_out, key_cache, value_cache, kv_length, cand_rows, final_gain[None, :],
        frequency, pick,
    )
    return (
        hidden_out.reshape(row_count // n, step_count, width),
        cand_logprob.reshape(CAP, step_count * cands),
    )


def solution(mesh):
    placed = (
        P("parts", None, "tp"),
        P("tp"),
        P(None, "tp"),
        P(None, "tp"),
        P(None, "tp"),
        P("tp", None),
        P(),
        P(),
        P("tp", None),
        P("tp", None),
        P("tp", None),
        P(None, "tp"),
        P(None, "tp"),
        P(None, "tp"),
        P("tp", None),
        P(None, "tp"),
        P(("parts", "tp"), None, None),
        P(("parts", "tp"), None, None),
        P(("parts", "tp")),
        P(("parts", "tp"), None, None),
        P(),
        P("parts", None),
    )
    return jax.shard_map(
        fused_on_device if mesh.shape["tp"] == FUSED_TP else on_device,
        mesh=mesh,
        in_specs=placed,
        out_specs=(P(("parts", "tp"), None, None), P(("parts", "tp"), None)),
        check_vma=False,
    )
```

```python
import math

import jax
import jax.numpy as jnp
import numpy as np
from jax import lax
from jax.experimental import pallas as pl
from jax.experimental.pallas import tpu as pltpu
from jax.sharding import PartitionSpec as P

CAP = 4


EPSILON = 1e-06
ROPE_BASE = 1000000.0


def scale_of(values):
    return lax.rsqrt(jnp.mean(values * values, axis=-1, keepdims=True) + EPSILON)


def rotary(values, position):
    half_size = values.shape[-1] // 2
    frequency = ROPE_BASE ** (-jnp.arange(half_size, dtype=jnp.float32) / half_size)
    angles = position.astype(jnp.float32)[:, :, None, None] * frequency
    angles = jnp.concatenate([angles, angles], axis=-1)
    turned = jnp.concatenate([-values[..., half_size:], values[..., :half_size]], axis=-1)
    return values * jnp.cos(angles) + turned * jnp.sin(angles)


def head_norm(values, gain_vec, position):
    floated = values.astype(jnp.float32)
    return rotary(floated * scale_of(floated) * gain_vec.astype(jnp.float32), position).astype(
        jnp.bfloat16
    )


def live_mask(lengths, span_len, step_count):
    column = jnp.arange(span_len + step_count, dtype=jnp.int32)[None, None, :]
    step_ids = jnp.arange(step_count, dtype=jnp.int32)[None, :, None]
    cached = (column < lengths[:, None, None]) & (column < span_len)
    fresh = (column >= span_len) & (column - span_len <= step_ids)
    return (cached | fresh).astype(jnp.float32)


def slot_of(row_owner, shards, capacity):
    owned_rows = (row_owner[:, None] == jnp.arange(shards, dtype=jnp.int32)[None, :]).astype(
        jnp.int32
    )
    before = jnp.cumsum(owned_rows, axis=0) - owned_rows
    return row_owner * capacity + jnp.sum(before * owned_rows, axis=1)


def exact_dot(left, right):
    return jnp.dot(left, right.astype(jnp.float32), precision=lax.Precision.HIGHEST)


def attend(queries, new_keys, new_values, key_cache, value_cache, lengths):
    row_count, step_count, head_count, head_size = queries.shape
    group_count = new_keys.shape[2]
    span_len = key_cache.shape[1]
    key_all = jnp.concatenate(
        [key_cache, new_keys.reshape(row_count, step_count, group_count * head_size)], axis=1
    )
    value_all = jnp.concatenate([value_cache, new_values], axis=1)
    key_all = key_all.reshape(row_count, span_len + step_count, group_count, head_size)
    value_all = value_all.reshape(row_count, span_len + step_count, group_count, head_size)
    grouped = queries.reshape(
        row_count, step_count, group_count, head_count // group_count, head_size
    )
    scores = jnp.einsum(
        "rsngd,rtnd->rsngt", grouped, key_all, preferred_element_type=jnp.float32
    ) / math.sqrt(head_size)
    weights = jnp.exp(scores) * live_mask(lengths, span_len, step_count)[:, :, None, None, :]
    weights = (weights / jnp.sum(weights, axis=-1, keepdims=True)).astype(jnp.bfloat16)
    mixed_heads = jnp.einsum(
        "rsngt,rtnd->rsngd", weights, value_all, preferred_element_type=jnp.float32
    )
    return mixed_heads.reshape(row_count, step_count, head_count * head_size).astype(jnp.bfloat16)


def on_device(
    x_in,
    ln_gain,
    w_query,
    w_key,
    w_value,
    w_out,
    q_gain,
    k_gain,
    a_query,
    a_key,
    a_value,
    b_query,
    b_key,
    b_value,
    a_out,
    b_out,
    key_cache,
    value_cache,
    kv_length,
    cand_rows,
    final_gain,
    row_owner,
):
    shards = lax.axis_size("tp")
    device_index = lax.axis_index("tp")
    row_count, step_count, part_width = x_in.shape
    full_width = part_width * shards
    local_rows = row_count // shards
    head_size = q_gain.shape[0]
    head_cols = w_query.shape[1]
    kv_cols = w_key.shape[1]
    rank_size = a_query.shape[1]
    x_float = x_in.astype(jnp.float32)
    squares = lax.psum(jnp.sum(x_float * x_float, axis=-1), "tp")
    inverse = lax.rsqrt(squares / full_width + EPSILON)[..., None]
    normed = (x_float * inverse * ln_gain.astype(jnp.float32)).astype(jnp.bfloat16)
    flat_normed = normed.reshape(row_count * step_count, part_width)
    base_weight = jnp.concatenate([w_query, w_key, w_value], axis=1)
    partial_low = jnp.concatenate(
        [
            jnp.dot(flat_normed, a_query, preferred_element_type=jnp.float32),
            jnp.dot(flat_normed, a_key, preferred_element_type=jnp.float32),
            jnp.dot(flat_normed, a_value, preferred_element_type=jnp.float32),
        ],
        axis=1,
    )
    low_full = lax.psum(partial_low, "tp")
    weight_parts = (base_weight,)
    lifted = jnp.concatenate(
        [
            exact_dot(low_full[:, :rank_size], b_query),
            exact_dot(low_full[:, rank_size : 2 * rank_size], b_key),
            exact_dot(low_full[:, 2 * rank_size :], b_value),
        ],
        axis=1,
    )
    part_weight = weight_parts[0]
    running = jnp.dot(
        lax.all_gather(flat_normed, "tp", axis=1, tiled=True),
        part_weight,
        preferred_element_type=jnp.float32,
    )
    projected = running + lifted
    mixed_proj = projected.astype(jnp.bfloat16).reshape(
        row_count, step_count, head_cols + 2 * kv_cols
    )
    by_row = lax.all_to_all(mixed_proj, "tp", split_axis=0, concat_axis=2, tiled=True)
    by_row = by_row.reshape(local_rows, step_count, shards, head_cols + 2 * kv_cols)
    query_lin = by_row[..., :head_cols].reshape(local_rows, step_count, -1, head_size)
    key_lin = by_row[..., head_cols : head_cols + kv_cols].reshape(
        local_rows, step_count, -1, head_size
    )
    value_lin = by_row[..., head_cols + kv_cols :].reshape(local_rows, step_count, shards * kv_cols)
    position = kv_length[:, None] + jnp.arange(step_count, dtype=jnp.int32)[None, :]
    queries = head_norm(query_lin, q_gain, position)
    new_keys = head_norm(key_lin, k_gain, position)
    attended = attend(queries, new_keys, value_lin, key_cache, value_cache, kv_length)
    by_head = lax.all_to_all(attended, "tp", split_axis=2, concat_axis=0, tiled=True)
    up_full = lax.all_gather(b_out, "tp", axis=1, tiled=True)
    segment = by_head.reshape(lax.axis_size("tp") * local_rows * step_count, head_cols)
    summed = lax.psum_scatter(
        (
            jnp.dot(segment, w_out, preferred_element_type=jnp.float32)
            + exact_dot(jnp.dot(segment, a_out, preferred_element_type=jnp.float32), up_full)
        ).reshape(lax.axis_size("tp") * local_rows, step_count, full_width),
        "tp",
        scatter_dimension=0,
        tiled=True,
    )
    residual = lax.all_to_all(x_in, "tp", split_axis=0, concat_axis=2, tiled=True)
    hidden_out = (residual.astype(jnp.float32) + summed).astype(jnp.bfloat16)
    hidden_float = hidden_out.astype(jnp.float32)
    final_normed = (hidden_float * scale_of(hidden_float) * final_gain.astype(jnp.float32)).astype(
        jnp.bfloat16
    )
    logits = jnp.einsum("rsd,rkd->rsk", final_normed, cand_rows, preferred_element_type=jnp.float32)
    logprob = logits - jnp.log(jnp.sum(jnp.exp(logits), axis=-1, keepdims=True))
    logprob = logprob.reshape(local_rows, step_count * cand_rows.shape[1])
    slot_index = slot_of(row_owner[:, 0], shards, CAP)
    all_rows = lax.all_gather(logprob, "tp", axis=0, tiled=True)
    wanted = device_index * CAP + jnp.arange(CAP, dtype=jnp.int32)
    select = (slot_index[None, :] == wanted[:, None]).astype(jnp.float32)
    cand_logprob = jnp.dot(select, all_rows, precision=lax.Precision.HIGHEST)
    return (hidden_out, cand_logprob)


MESH = pl.DeviceIdType.MESH
NZ, NY, NC = 4, 2, 2
FUSED_TP = NZ * NY * NC
CHUNKS = 4
F32, BF16 = jnp.float32, jnp.bfloat16


def dot_nt(left, right):
    return lax.dot_general(left, right, (((1,), (1,)), ((), ())), preferred_element_type=F32)


def dot_nn(left, right):
    return jnp.dot(left, right, preferred_element_type=F32)


def split_high_low(values):
    high = values.astype(BF16)
    return high, (values - high.astype(F32)).astype(BF16)


def fused_kernel(
    x_ref, gain_ref, wq_hbm, wk_hbm, wv_hbm, wo_hbm, qg_ref, kg_ref, aq_ref, ak_ref, av_ref,
    bq_hbm, bk_ref, bv_ref, ao_hbm, bo_ref, kc_hbm, vc_hbm, len_ref, cand_hbm, fg_ref, freq_ref,
    owner_ref,
    hid_ref, lp_ref,
    wq, wkv, wo, keys, vals, xall, ball, lowp, lowr, lowall, upm, accq, acckv, xres, bfull,
    bq_ref, ao_ref, cand_ref, pick, projs, projr, atts, attr, parts, got_c, half_y, got_y, quarter, got_z, hidden, lpall,
    local_sem, xs, xr, bs, br, l1s, l1r, l2s, l2r, ps, pr, ats, atr,
    cs, cr, ys, yr, zs, zr, gs, gr,
):
    n = FUSED_TP
    me = lax.axis_index("tp")
    core, y, z = lax.rem(me, NC), lax.rem(me // NC, NY), me // (NC * NY)
    row_count, steps, part = x_ref.shape
    groups, rows8 = n, row_count * steps // n
    width = part * n
    rank = aq_ref.shape[0]
    span = kc_hbm.shape[1]
    padded = keys.shape[1]
    head = qg_ref.shape[1]
    qcols = wq.shape[1]
    rows = groups * rows8
    chunk = width // CHUNKS

    def place(pz, py, pc):
        return (pz * NY + py) * NC + pc

    y_peer, c_peer = place(z, 1 - y, core), place(z, y, 1 - core)

    def remote(source, target, send, recv, device):
        return pltpu.make_async_remote_copy(
            src_ref=source, dst_ref=target, send_sem=send, recv_sem=recv,
            device_id={"tp": device}, device_id_type=MESH,
        )

    loads = [
        pltpu.make_async_copy(wq_hbm, wq, local_sem.at[0]),
        pltpu.make_async_copy(wk_hbm, wkv.at[pl.ds(0, wk_hbm.shape[0])], local_sem.at[1]),
        pltpu.make_async_copy(wv_hbm, wkv.at[pl.ds(wk_hbm.shape[0], wk_hbm.shape[0])], local_sem.at[2]),
        pltpu.make_async_copy(kc_hbm.at[0], keys.at[0, pl.ds(0, span)], local_sem.at[3]),
        pltpu.make_async_copy(kc_hbm.at[1], keys.at[1, pl.ds(0, span)], local_sem.at[4]),
        pltpu.make_async_copy(vc_hbm.at[0], vals.at[0, pl.ds(0, span)], local_sem.at[5]),
        pltpu.make_async_copy(vc_hbm.at[1], vals.at[1, pl.ds(0, span)], local_sem.at[6]),
        pltpu.make_async_copy(wo_hbm, wo, local_sem.at[7]),
        pltpu.make_async_copy(bq_hbm, bq_ref, local_sem.at[8]),
        pltpu.make_async_copy(ao_hbm, ao_ref, local_sem.at[9]),
        pltpu.make_async_copy(cand_hbm, cand_ref, local_sem.at[10]),
    ]
    for load in loads:
        load.start()

    barrier = pltpu.get_barrier_semaphore()

    def greet(d, carry):
        pl.semaphore_signal(barrier, inc=1, device_id={"tp": lax.rem(me + d, n)}, device_id_type=MESH)
        return carry

    lax.fori_loop(1, n, greet, 0)

    own = x_ref[...].astype(F32).reshape(rows, part)
    gain_row = gain_ref[...].astype(F32)[None, :]
    xall[me, 0:groups] = own.reshape(groups, rows8, part).astype(BF16)
    xall[me, groups] = jnp.broadcast_to(gain_row, (rows8, part)).astype(BF16)
    ball[me] = bo_ref[...]
    pl.semaphore_wait(barrier, n - 1)

    def gather(buffer, send, recv):
        def hop(block, device, number):
            return remote(buffer.at[block], buffer.at[block], send.at[number], recv.at[block], device)

        def begin():
            hop(me, y_peer, 0).start()
            for dz in range(1, NZ):
                hop(me, place(lax.rem(z + dz, NZ), y, core), dz).start()
            hop(me, c_peer, NZ).start()

        def middle():
            for dz in range(1, NZ):
                block = place(lax.rem(z + dz, NZ), y, core)
                hop(block, y_peer, 0).wait_recv()
                hop(block, y_peer, NZ + dz).start()
                hop(block, c_peer, 2 * NZ - 1 + dz).start()

        def late():
            for dz in range(NZ):
                block = place(lax.rem(z + dz, NZ), 1 - y, core)
                hop(block, c_peer, 0).wait_recv()
                hop(block, c_peer, 3 * NZ - 1 + dz).start()

        def finish():
            for dz in range(NZ):
                for py in range(NY):
                    hop(place(lax.rem(z + dz, NZ), py, 1 - core), c_peer, 0).wait_recv()

        def drain():
            for number in range(n - 1):
                hop(me, c_peer, number).wait_send()

        return begin, middle, late, finish, drain

    def exchange(source, target, send, recv, spread):
        def copy(to, slot, device):
            part_of = source.at[me] if spread else source.at[to]
            return remote(part_of, target.at[slot], send.at[to], recv.at[slot], device)

        def begin():
            def one(d, carry):
                to = lax.rem(me + d, n)
                copy(to, me, to).start()
                return carry

            lax.fori_loop(1, n, one, 0)

        def finish():
            def one(d, carry):
                other = lax.rem(me + d, n)
                copy(other, other, other).wait_recv()
                return carry

            lax.fori_loop(1, n, one, 0)

        def drain():
            def one(d, carry):
                other = lax.rem(me + d, n)
                copy(other, other, other).wait_send()
                return carry

            lax.fori_loop(1, n, one, 0)

        return begin, finish, drain

    x_gather = gather(xall, xs, xr)
    b_gather = gather(ball, bs, br)
    low_scatter = exchange(lowp, lowr, l1s, l1r, False)
    low_spread = exchange(lowall, lowall, l2s, l2r, True)
    proj_swap = exchange(projs, projr, ps, pr, False)
    att_swap = exchange(atts, attr, ats, atr, False)
    lp_spread = exchange(lpall, lpall, gs, gr, True)

    x_gather[0]()

    own_gained = (own * gain_row).astype(BF16)
    down = jnp.concatenate([aq_ref[...], ak_ref[...], av_ref[...], jnp.zeros((rank, part), BF16)], axis=0)
    low_part = dot_nt(own_gained, down)
    square = jnp.sum(own * own, axis=-1, keepdims=True)
    lane = lax.broadcasted_iota(jnp.int32, low_part.shape, 1)
    lowp[...] = jnp.where(lane < 3 * rank, low_part, square).reshape(lowp.shape)
    lowr[me] = lowp[me]
    low_scatter[0]()

    loads[8].wait()
    upm[...] = jnp.zeros_like(upm)
    upm[0:rank, 0:qcols] = bq_ref[...]
    empty = jnp.zeros(bk_ref.shape, F32)
    upm[rank : 2 * rank, qcols:] = jnp.concatenate([bk_ref[...].astype(F32), empty], axis=1).astype(BF16)
    upm[2 * rank : 3 * rank, qcols:] = jnp.concatenate([empty, bv_ref[...].astype(F32)], axis=1).astype(BF16)
    for r in range(2):
        keys[r, span:padded] = jnp.zeros((padded - span, keys.shape[2]), BF16)
        vals[r, span:padded] = jnp.zeros((padded - span, vals.shape[2]), BF16)
    sub8 = lax.broadcasted_iota(jnp.int32, (rows8, head), 0)
    lane8 = lax.broadcasted_iota(jnp.int32, (rows8, head), 1)
    position = jnp.where(sub8 < steps, len_ref[0] + sub8, len_ref[1] + sub8 - steps).astype(F32)
    angle = position * freq_ref[...]
    cosine = jnp.cos(angle)[None]
    sine = jnp.sin(angle)
    sine = jnp.where(lane8 < head // 2, -sine, sine)[None]

    sub_pick = lax.broadcasted_iota(jnp.int32, pick.shape, 0)
    row_pick = lax.broadcasted_iota(jnp.int32, pick.shape, 1) // steps
    chosen = jnp.zeros(pick.shape, F32)
    owned = jnp.int32(0)
    for row in range(row_count):
        mine = (owner_ref[row] == me).astype(jnp.int32)
        chosen = chosen + jnp.where((sub_pick == owned) & (row_pick == row), mine, 0).astype(F32)
        owned = owned + mine
    pick[...] = chosen

    x_gather[1]()
    low_scatter[1]()
    lowall[me] = jnp.sum(lowr[...], axis=0)
    low_spread[0]()
    x_gather[2]()
    for load in loads[:3]:
        load.wait()
    x_gather[3]()
    b_gather[0]()

    pair = NC * part
    for m in range(n // 2):
        sides, kept = [], []
        for b in (2 * m, 2 * m + 1):
            block = xall[b, 0:groups].astype(F32).reshape(rows, part)
            sides.append(block * xall[b, groups].astype(F32)[0:1])
            kept.append(xall[b, me].astype(F32))
        gained = jnp.concatenate(sides, axis=1).astype(BF16)
        xres[:, m * pair : (m + 1) * pair] = jnp.concatenate(kept, axis=1)
        more_q = dot_nn(gained, wq[m * pair : (m + 1) * pair, :])
        more_kv = dot_nt(gained, wkv[:, m * pair : (m + 1) * pair])
        accq[...] = more_q if m == 0 else accq[...] + more_q
        acckv[...] = more_kv if m == 0 else acckv[...] + more_kv

    low_spread[1]()
    low_all = lowall[...].reshape(rows, lowall.shape[2])
    inverse = lax.rsqrt(low_all[:, 3 * rank : 3 * rank + 1] / width + EPSILON)
    low_high, low_low = split_high_low(jnp.where(lane < 3 * rank, low_all * inverse, 0.0))
    lifted = dot_nn(low_high, upm[...]) + dot_nn(low_low, upm[...])
    projs[:, :, 0:qcols] = (accq[...] * inverse + lifted[:, 0:qcols]).reshape(groups, rows8, qcols).astype(BF16)
    projs[:, :, qcols:] = (acckv[...] * inverse + lifted[:, qcols:]).reshape(groups, rows8, head).astype(BF16)
    projr[me] = projs[me]
    proj_swap[0]()
    proj_swap[1]()
    b_gather[1]()

    def normed_heads(values, gain_row):
        scaled = values * lax.rsqrt(jnp.mean(values * values, axis=-1, keepdims=True) + EPSILON)
        scaled = scaled * gain_row[...].astype(F32)[None]
        return scaled * cosine + pltpu.roll(scaled, head // 2, 2) * sine

    sub16 = lax.broadcasted_iota(jnp.int32, (n, rows8, head), 1)
    by_row = [[], []]
    for p in range(qcols // (2 * head)):
        first = normed_heads(projr[:, :, 2 * p * head : (2 * p + 1) * head].astype(F32), qg_ref)
        second = normed_heads(projr[:, :, (2 * p + 1) * head : (2 * p + 2) * head].astype(F32), qg_ref)
        by_row[0].append(jnp.where(sub16 < steps, first, pltpu.roll(second, steps, 1)))
        by_row[1].append(jnp.where(sub16 < steps, pltpu.roll(first, steps, 1), second))
    kv_groups = n // 2
    kv_all = projr[:, :, qcols:].astype(F32).reshape(kv_groups, 2, rows8, head)
    even, odd = kv_all[:, 0], kv_all[:, 1]
    lane_kv = lax.broadcasted_iota(jnp.int32, even.shape, 2)
    new_keys = normed_heads(jnp.where(lane_kv < head // 2, even, pltpu.roll(odd, head // 2, 2)), kg_ref)
    new_vals = jnp.where(lane_kv < head // 2, pltpu.roll(even, head // 2, 2), odd)

    for load in loads[3:7]:
        load.wait()
    blank = jnp.zeros((rows8, head), F32)
    for g in range(kv_groups):
        new_key = jnp.concatenate([new_keys[g], blank], axis=0).astype(BF16)
        new_val = jnp.concatenate([new_vals[g], blank], axis=0).astype(BF16)
        for r in range(2):
            keys[r, span : span + 2 * rows8, g * head : (g + 1) * head] = new_key
            vals[r, span : span + 2 * rows8, g * head : (g + 1) * head] = new_val

    asked = 4 * rows8
    column = lax.broadcasted_iota(jnp.int32, (asked, padded), 1)
    step_of = lax.rem(lax.broadcasted_iota(jnp.int32, (asked, padded), 0), steps)
    live = []
    for r in range(2):
        fresh = column - span - r * steps
        in_cache = (column < len_ref[r]) & (column < span)
        live.append((in_cache | ((fresh >= 0) & (fresh <= step_of) & (column >= span))).astype(F32))
    sub4 = lax.broadcasted_iota(jnp.int32, (4, rows8, head), 1)
    for g in range(kv_groups):
        outs = []
        for r in range(2):
            tiles = [by_row[r][p][2 * g + side][None] for side in range(2) for p in range(2)]
            query = jnp.concatenate(tiles, axis=0).reshape(asked, head).astype(BF16)
            scores = dot_nt(query, keys[r, :, g * head : (g + 1) * head]) * (1.0 / math.sqrt(head))
            weights = jnp.exp(scores) * live[r]
            total = jnp.sum(weights, axis=-1, keepdims=True)
            mixed = dot_nn(weights.astype(BF16), vals[r, :, g * head : (g + 1) * head]) / total
            outs.append(mixed.reshape(4, rows8, head))
        first = jnp.where(sub4 < steps, outs[0], pltpu.roll(outs[1], steps, 1)).astype(BF16)
        second = jnp.where(sub4 < steps, pltpu.roll(outs[0], steps, 1), outs[1]).astype(BF16)
        for side in range(2):
            for p in range(2):
                atts[2 * g + side, :, 2 * p * head : (2 * p + 1) * head] = first[2 * side + p]
                atts[2 * g + side, :, (2 * p + 1) * head : (2 * p + 2) * head] = second[2 * side + p]
    attr[me] = atts[me]
    att_swap[0]()
    b_gather[2]()
    b_gather[3]()
    for m in range(n // 2):
        bfull[:, m * pair : (m + 1) * pair] = jnp.concatenate(
            [ball[2 * m].astype(F32), ball[2 * m + 1].astype(F32)], axis=1
        ).astype(BF16)
    for load in (loads[7], loads[9], loads[10]):
        load.wait()
    att_swap[1]()

    segment = attr[...].astype(F32).reshape(rows, qcols).astype(BF16)
    inner_high, inner_low = split_high_low(dot_nt(segment, ao_ref[...]))

    def c_hop(k):
        return remote(parts.at[k, 1 - core], got_c.at[k], cs.at[k], cr.at[k], c_peer)

    def y_hop(k):
        return remote(half_y.at[k, 1 - y], got_y.at[k], ys.at[k], yr.at[k], y_peer)

    def z_hop(k, dz):
        other = lax.rem(z + dz, NZ)
        return remote(quarter.at[k, other], got_z.at[k, dz - 1], zs.at[k, dz - 1], zr.at[k, dz - 1], place(other, y, core))

    def multiply(k):
        at = slice(k * chunk, (k + 1) * chunk)
        up = bfull[:, at]
        out = dot_nn(segment, wo[:, at]) + (dot_nn(inner_high, up) + dot_nn(inner_low, up))
        out = out.reshape(groups // NC, NC, rows8, chunk).astype(BF16)
        for pc in range(NC):
            parts[k, pc] = out[:, pc]
        c_hop(k).start()

    def over_y(k):
        c_hop(k).wait_recv()
        both = parts[k, core].astype(F32) + got_c[k].astype(F32)
        both = both.reshape(NZ, NY, rows8, chunk).astype(BF16)
        for py in range(NY):
            half_y[k, py] = both[:, py]
        y_hop(k).start()

    def over_z(k):
        y_hop(k).wait_recv()
        quarter[k] = (half_y[k, y].astype(F32) + got_y[k].astype(F32)).astype(BF16)
        for dz in range(1, NZ):
            z_hop(k, dz).start()

    for k in range(CHUNKS):
        multiply(k)
        if k >= 1:
            over_y(k - 1)
    over_y(CHUNKS - 1)
    for k in range(CHUNKS):
        over_z(k)

    squares = jnp.zeros((rows8, 1), F32)
    for k in range(CHUNKS):
        at = slice(k * chunk, (k + 1) * chunk)
        total = xres[:, at] + quarter[k, z].astype(F32)
        for dz in range(1, NZ):
            z_hop(k, dz).wait_recv()
            total = total + got_z[k, dz - 1].astype(F32)
        rounded = total.astype(BF16)
        rounded = rounded.astype(F32)
        for row in range(2):
            hid_ref[row, :, at] = rounded[row * steps : (row + 1) * steps].astype(BF16)
        hidden[:, at] = rounded
        squares = squares + jnp.sum(rounded * rounded, axis=-1, keepdims=True)
    final = (hidden[...] * lax.rsqrt(squares / width + EPSILON) * fg_ref[...].astype(F32)[None, :]).astype(BF16)
    cands = cand_ref.shape[1]
    logits = jnp.where(
        lax.broadcasted_iota(jnp.int32, (rows8, cands), 0) < steps,
        dot_nt(final, cand_ref[0]),
        dot_nt(final, cand_ref[1]),
    )
    logprob = logits - jnp.log(jnp.sum(jnp.exp(logits), axis=-1, keepdims=True))
    spaced = jnp.concatenate(
        [logprob] * steps + [jnp.zeros((rows8, lpall.shape[2] - steps * cands), F32)], axis=1
    )
    lane_lp = lax.broadcasted_iota(jnp.int32, spaced.shape, 1)
    step_lp = lax.rem(lax.broadcasted_iota(jnp.int32, spaced.shape, 0), steps)
    lpall[me] = jnp.where(lane_lp // cands == step_lp, spaced, 0.0)
    lp_spread[0]()
    lp_spread[1]()
    placed = jnp.dot(
        pick[...], lpall[...].reshape(rows, lpall.shape[2]),
        precision=lax.Precision.HIGHEST, preferred_element_type=F32,
    )
    lp_ref[...] = placed[0 : lp_ref.shape[0], 0 : lp_ref.shape[1]]

    x_gather[4]()
    b_gather[4]()
    for swap in (low_scatter, low_spread, proj_swap, att_swap, lp_spread):
        swap[2]()
    for k in range(CHUNKS):
        c_hop(k).wait_send()
        y_hop(k).wait_send()
        for dz in range(1, NZ):
            z_hop(k, dz).wait_send()


def fused_on_device(
    x_in, ln_gain, w_query, w_key, w_value, w_out, q_gain, k_gain, a_query, a_key, a_value,
    b_query, b_key, b_value, a_out, b_out, key_cache, value_cache, kv_length, cand_rows,
    final_gain, row_owner,
):
    n = lax.axis_size("tp")
    me = lax.axis_index("tp")
    row_count, step_count, part = x_in.shape
    rows8 = row_count * step_count // n
    width = part * n
    head = q_gain.shape[0]
    qcols = w_query.shape[1]
    kvcols = w_key.shape[1]
    cols = qcols + 2 * kvcols
    rank = a_query.shape[1]
    span, kv_width = key_cache.shape[1:]
    cands = cand_rows.shape[1]
    half = head // 2
    frequency = ROPE_BASE ** (-np.arange(half, dtype=np.float32) / np.float32(half))
    frequency = jnp.asarray(np.concatenate([frequency, frequency])[None, :].astype(np.float32))

    chunk = width // CHUNKS
    rows = row_count * step_count
    padded = span + 128
    vmem = pl.BlockSpec(memory_space=pltpu.VMEM)
    smem = pl.BlockSpec(memory_space=pltpu.SMEM)
    hbm = pl.BlockSpec(memory_space=pl.ANY)
    dma = pltpu.SemaphoreType.DMA
    return pl.pallas_call(
        fused_kernel,
        out_shape=(
            jax.ShapeDtypeStruct((row_count // n, step_count, width), BF16),
            jax.ShapeDtypeStruct((CAP, step_count * cands), F32),
        ),
        in_specs=[vmem, vmem, hbm, hbm, hbm, hbm, vmem, vmem, vmem, vmem, vmem,
                  hbm, vmem, vmem, hbm, vmem, hbm, hbm, smem, hbm, vmem, vmem, smem],
        out_specs=(vmem, vmem),
        scratch_shapes=[
            pltpu.VMEM((width, qcols), BF16),
            pltpu.VMEM((2 * kvcols, width), BF16),
            pltpu.VMEM((qcols, width), BF16),
            pltpu.VMEM((2, padded, kv_width), BF16),
            pltpu.VMEM((2, padded, kv_width), BF16),
            pltpu.VMEM((n, n + 1, rows8, part), BF16),
            pltpu.VMEM((n, rank, part), BF16),
            pltpu.VMEM((n, rows8, 4 * rank), F32),
            pltpu.VMEM((n, rows8, 4 * rank), F32),
            pltpu.VMEM((n, rows8, 4 * rank), F32),
            pltpu.VMEM((4 * rank, cols), BF16),
            pltpu.VMEM((rows, qcols), F32),
            pltpu.VMEM((rows, 2 * kvcols), F32),
            pltpu.VMEM((rows8, width), F32),
            pltpu.VMEM((rank, width), BF16),
            pltpu.VMEM(b_query.shape, BF16),
            pltpu.VMEM((rank, qcols), BF16),
            pltpu.VMEM(cand_rows.shape, BF16),
            pltpu.VMEM((8, rows), F32),
            pltpu.VMEM((n, rows8, cols), BF16),
            pltpu.VMEM((n, rows8, cols), BF16),
            pltpu.VMEM((n, rows8, qcols), BF16),
            pltpu.VMEM((n, rows8, qcols), BF16),
            pltpu.VMEM((CHUNKS, NC, NZ * NY, rows8, chunk), BF16),
            pltpu.VMEM((CHUNKS, NZ * NY, rows8, chunk), BF16),
            pltpu.VMEM((CHUNKS, NY, NZ, rows8, chunk), BF16),
            pltpu.VMEM((CHUNKS, NZ, rows8, chunk), BF16),
            pltpu.VMEM((CHUNKS, NZ, rows8, chunk), BF16),
            pltpu.VMEM((CHUNKS, NZ - 1, rows8, chunk), BF16),
            pltpu.VMEM((rows8, width), F32),
            pltpu.VMEM((n, rows8, 128), F32),
            dma((11,)),
            dma((n,)), dma((n,)), dma((n,)), dma((n,)),
            dma((n,)), dma((n,)), dma((n,)), dma((n,)),
            dma((n,)), dma((n,)), dma((n,)), dma((n,)),
            dma((CHUNKS,)), dma((CHUNKS,)), dma((CHUNKS,)), dma((CHUNKS,)),
            dma((CHUNKS, NZ - 1)), dma((CHUNKS, NZ - 1)),
            dma((n,)), dma((n,)),
        ],
        compiler_params=pltpu.CompilerParams(
            collective_id=0, has_side_effects=True, vmem_limit_bytes=56 * 1024 * 1024
        ),
        name="layer",
    )(
        x_in, ln_gain, w_query, w_key.T, w_value.T, w_out,
        q_gain[None, :], k_gain[None, :], a_query.T, a_key.T, a_value.T, b_query, b_key, b_value,
        a_out.T, b_out, key_cache, value_cache, kv_length, cand_rows, final_gain,
        frequency, row_owner[:, 0],
    )


def solution(mesh):
    placed = (
        P("parts", None, "tp"),
        P("tp"),
        P(None, "tp"),
        P(None, "tp"),
        P(None, "tp"),
        P("tp", None),
        P(),
        P(),
        P("tp", None),
        P("tp", None),
        P("tp", None),
        P(None, "tp"),
        P(None, "tp"),
        P(None, "tp"),
        P("tp", None),
        P(None, "tp"),
        P(("parts", "tp"), None, None),
        P(("parts", "tp"), None, None),
        P(("parts", "tp")),
        P(("parts", "tp"), None, None),
        P(),
        P("parts", None),
    )
    return jax.shard_map(
        fused_on_device if mesh.shape["tp"] == FUSED_TP else on_device,
        mesh=mesh,
        in_specs=placed,
        out_specs=(P(("parts", "tp"), None, None), P(("parts", "tp"), None)),
        check_vma=False,
    )
```

```python
import math

import jax
import jax.numpy as jnp
import numpy as np
from jax import lax
from jax.experimental import pallas as pl
from jax.experimental.pallas import tpu as pltpu
from jax.sharding import PartitionSpec as P

CAP = 4


EPSILON = 1e-06
ROPE_BASE = 1000000.0


def scale_of(values):
    return lax.rsqrt(jnp.mean(values * values, axis=-1, keepdims=True) + EPSILON)


def rotary(values, position):
    half_size = values.shape[-1] // 2
    frequency = ROPE_BASE ** (-jnp.arange(half_size, dtype=jnp.float32) / half_size)
    angles = position.astype(jnp.float32)[:, :, None, None] * frequency
    angles = jnp.concatenate([angles, angles], axis=-1)
    turned = jnp.concatenate([-values[..., half_size:], values[..., :half_size]], axis=-1)
    return values * jnp.cos(angles) + turned * jnp.sin(angles)


def head_norm(values, gain_vec, position):
    floated = values.astype(jnp.float32)
    return rotary(floated * scale_of(floated) * gain_vec.astype(jnp.float32), position).astype(
        jnp.bfloat16
    )


def live_mask(lengths, span_len, step_count):
    column = jnp.arange(span_len + step_count, dtype=jnp.int32)[None, None, :]
    step_ids = jnp.arange(step_count, dtype=jnp.int32)[None, :, None]
    cached = (column < lengths[:, None, None]) & (column < span_len)
    fresh = (column >= span_len) & (column - span_len <= step_ids)
    return (cached | fresh).astype(jnp.float32)


def slot_of(row_owner, shards, capacity):
    owned_rows = (row_owner[:, None] == jnp.arange(shards, dtype=jnp.int32)[None, :]).astype(
        jnp.int32
    )
    before = jnp.cumsum(owned_rows, axis=0) - owned_rows
    return row_owner * capacity + jnp.sum(before * owned_rows, axis=1)


def exact_dot(left, right):
    return jnp.dot(left, right.astype(jnp.float32), precision=lax.Precision.HIGHEST)


def attend(queries, new_keys, new_values, key_cache, value_cache, lengths):
    row_count, step_count, head_count, head_size = queries.shape
    group_count = new_keys.shape[2]
    span_len = key_cache.shape[1]
    key_all = jnp.concatenate(
        [key_cache, new_keys.reshape(row_count, step_count, group_count * head_size)], axis=1
    )
    value_all = jnp.concatenate([value_cache, new_values], axis=1)
    key_all = key_all.reshape(row_count, span_len + step_count, group_count, head_size)
    value_all = value_all.reshape(row_count, span_len + step_count, group_count, head_size)
    grouped = queries.reshape(
        row_count, step_count, group_count, head_count // group_count, head_size
    )
    scores = jnp.einsum(
        "rsngd,rtnd->rsngt", grouped, key_all, preferred_element_type=jnp.float32
    ) / math.sqrt(head_size)
    weights = jnp.exp(scores) * live_mask(lengths, span_len, step_count)[:, :, None, None, :]
    weights = (weights / jnp.sum(weights, axis=-1, keepdims=True)).astype(jnp.bfloat16)
    mixed_heads = jnp.einsum(
        "rsngt,rtnd->rsngd", weights, value_all, preferred_element_type=jnp.float32
    )
    return mixed_heads.reshape(row_count, step_count, head_count * head_size).astype(jnp.bfloat16)


def on_device(
    x_in,
    ln_gain,
    w_query,
    w_key,
    w_value,
    w_out,
    q_gain,
    k_gain,
    a_query,
    a_key,
    a_value,
    b_query,
    b_key,
    b_value,
    a_out,
    b_out,
    key_cache,
    value_cache,
    kv_length,
    cand_rows,
    final_gain,
    row_owner,
):
    shards = lax.axis_size("tp")
    device_index = lax.axis_index("tp")
    row_count, step_count, part_width = x_in.shape
    full_width = part_width * shards
    local_rows = row_count // shards
    head_size = q_gain.shape[0]
    head_cols = w_query.shape[1]
    kv_cols = w_key.shape[1]
    rank_size = a_query.shape[1]
    x_float = x_in.astype(jnp.float32)
    squares = lax.psum(jnp.sum(x_float * x_float, axis=-1), "tp")
    inverse = lax.rsqrt(squares / full_width + EPSILON)[..., None]
    normed = (x_float * inverse * ln_gain.astype(jnp.float32)).astype(jnp.bfloat16)
    flat_normed = normed.reshape(row_count * step_count, part_width)
    base_weight = jnp.concatenate([w_query, w_key, w_value], axis=1)
    partial_low = jnp.concatenate(
        [
            jnp.dot(flat_normed, a_query, preferred_element_type=jnp.float32),
            jnp.dot(flat_normed, a_key, preferred_element_type=jnp.float32),
            jnp.dot(flat_normed, a_value, preferred_element_type=jnp.float32),
        ],
        axis=1,
    )
    low_full = lax.psum(partial_low, "tp")
    weight_parts = (base_weight,)
    lifted = jnp.concatenate(
        [
            exact_dot(low_full[:, :rank_size], b_query),
            exact_dot(low_full[:, rank_size : 2 * rank_size], b_key),
            exact_dot(low_full[:, 2 * rank_size :], b_value),
        ],
        axis=1,
    )
    part_weight = weight_parts[0]
    running = jnp.dot(
        lax.all_gather(flat_normed, "tp", axis=1, tiled=True),
        part_weight,
        preferred_element_type=jnp.float32,
    )
    projected = running + lifted
    mixed_proj = projected.astype(jnp.bfloat16).reshape(
        row_count, step_count, head_cols + 2 * kv_cols
    )
    by_row = lax.all_to_all(mixed_proj, "tp", split_axis=0, concat_axis=2, tiled=True)
    by_row = by_row.reshape(local_rows, step_count, shards, head_cols + 2 * kv_cols)
    query_lin = by_row[..., :head_cols].reshape(local_rows, step_count, -1, head_size)
    key_lin = by_row[..., head_cols : head_cols + kv_cols].reshape(
        local_rows, step_count, -1, head_size
    )
    value_lin = by_row[..., head_cols + kv_cols :].reshape(local_rows, step_count, shards * kv_cols)
    position = kv_length[:, None] + jnp.arange(step_count, dtype=jnp.int32)[None, :]
    queries = head_norm(query_lin, q_gain, position)
    new_keys = head_norm(key_lin, k_gain, position)
    attended = attend(queries, new_keys, value_lin, key_cache, value_cache, kv_length)
    by_head = lax.all_to_all(attended, "tp", split_axis=2, concat_axis=0, tiled=True)
    up_full = lax.all_gather(b_out, "tp", axis=1, tiled=True)
    segment = by_head.reshape(lax.axis_size("tp") * local_rows * step_count, head_cols)
    summed = lax.psum_scatter(
        (
            jnp.dot(segment, w_out, preferred_element_type=jnp.float32)
            + exact_dot(jnp.dot(segment, a_out, preferred_element_type=jnp.float32), up_full)
        ).reshape(lax.axis_size("tp") * local_rows, step_count, full_width),
        "tp",
        scatter_dimension=0,
        tiled=True,
    )
    residual = lax.all_to_all(x_in, "tp", split_axis=0, concat_axis=2, tiled=True)
    hidden_out = (residual.astype(jnp.float32) + summed).astype(jnp.bfloat16)
    hidden_float = hidden_out.astype(jnp.float32)
    final_normed = (hidden_float * scale_of(hidden_float) * final_gain.astype(jnp.float32)).astype(
        jnp.bfloat16
    )
    logits = jnp.einsum("rsd,rkd->rsk", final_normed, cand_rows, preferred_element_type=jnp.float32)
    logprob = logits - jnp.log(jnp.sum(jnp.exp(logits), axis=-1, keepdims=True))
    logprob = logprob.reshape(local_rows, step_count * cand_rows.shape[1])
    slot_index = slot_of(row_owner[:, 0], shards, CAP)
    all_rows = lax.all_gather(logprob, "tp", axis=0, tiled=True)
    wanted = device_index * CAP + jnp.arange(CAP, dtype=jnp.int32)
    select = (slot_index[None, :] == wanted[:, None]).astype(jnp.float32)
    cand_logprob = jnp.dot(select, all_rows, precision=lax.Precision.HIGHEST)
    return (hidden_out, cand_logprob)


MESH = pl.DeviceIdType.MESH
NZ, NY, NC = 4, 2, 2
FUSED_TP = NZ * NY * NC
CHUNKS = 4
F32, BF16 = jnp.float32, jnp.bfloat16


def dot_nt(left, right):
    return lax.dot_general(left, right, (((1,), (1,)), ((), ())), preferred_element_type=F32)


def dot_nn(left, right):
    return jnp.dot(left, right, preferred_element_type=F32)


def split_high_low(values):
    high = values.astype(BF16)
    return high, (values - high.astype(F32)).astype(BF16)


def fused_kernel(
    x_ref, gain_ref, wq_hbm, wk_hbm, wv_hbm, wo_hbm, qg_ref, kg_ref, aq_ref, ak_ref, av_ref,
    bq_hbm, bk_ref, bv_ref, ao_hbm, bo_ref, kc_hbm, vc_hbm, len_ref, cand_hbm, fg_ref, freq_ref,
    owner_ref,
    hid_ref, lp_ref,
    wq, wkv, wo, keys, vals, xall, ball, lowp, lowr, lowall, upm, accq, acckv, xres, bfull,
    bq_ref, ao_ref, cand_ref, pick, projs, projr, atts, attr, parts, got_c, half_y, got_y, quarter, got_z, hidden, lpall,
    local_sem, xs, xr, bs, br, l1s, l1r, l2s, l2r, ps, pr, ats, atr,
    cs, cr, ys, yr, zs, zr, gs, gr,
):
    n = FUSED_TP
    me = lax.axis_index("tp")
    core, y, z = lax.rem(me, NC), lax.rem(me // NC, NY), me // (NC * NY)
    row_count, steps, part = x_ref.shape
    groups, rows8 = n, row_count * steps // n
    width = part * n
    rank = aq_ref.shape[0]
    span = kc_hbm.shape[1]
    padded = keys.shape[1]
    head = qg_ref.shape[1]
    qcols = wq.shape[1]
    rows = groups * rows8
    chunk = width // CHUNKS

    def place(pz, py, pc):
        return (pz * NY + py) * NC + pc

    y_peer, c_peer = place(z, 1 - y, core), place(z, y, 1 - core)

    def remote(source, target, send, recv, device):
        return pltpu.make_async_remote_copy(
            src_ref=source, dst_ref=target, send_sem=send, recv_sem=recv,
            device_id={"tp": device}, device_id_type=MESH,
        )

    loads = [
        pltpu.make_async_copy(wq_hbm, wq, local_sem.at[0]),
        pltpu.make_async_copy(wk_hbm, wkv.at[pl.ds(0, wk_hbm.shape[0])], local_sem.at[1]),
        pltpu.make_async_copy(wv_hbm, wkv.at[pl.ds(wk_hbm.shape[0], wk_hbm.shape[0])], local_sem.at[2]),
        pltpu.make_async_copy(kc_hbm.at[0], keys.at[0, pl.ds(0, span)], local_sem.at[3]),
        pltpu.make_async_copy(kc_hbm.at[1], keys.at[1, pl.ds(0, span)], local_sem.at[4]),
        pltpu.make_async_copy(vc_hbm.at[0], vals.at[0, pl.ds(0, span)], local_sem.at[5]),
        pltpu.make_async_copy(vc_hbm.at[1], vals.at[1, pl.ds(0, span)], local_sem.at[6]),
        pltpu.make_async_copy(wo_hbm, wo, local_sem.at[7]),
        pltpu.make_async_copy(bq_hbm, bq_ref, local_sem.at[8]),
        pltpu.make_async_copy(ao_hbm, ao_ref, local_sem.at[9]),
        pltpu.make_async_copy(cand_hbm, cand_ref, local_sem.at[10]),
    ]
    for load in loads:
        load.start()

    barrier = pltpu.get_barrier_semaphore()

    def greet(d, carry):
        pl.semaphore_signal(barrier, inc=1, device_id={"tp": lax.rem(me + d, n)}, device_id_type=MESH)
        return carry

    lax.fori_loop(1, n, greet, 0)

    own = x_ref[...].astype(F32).reshape(rows, part)
    gain_row = gain_ref[...].astype(F32)[None, :]
    xall[me, 0:groups] = own.reshape(groups, rows8, part).astype(BF16)
    xall[me, groups] = jnp.broadcast_to(gain_row, (rows8, part)).astype(BF16)
    ball[me] = bo_ref[...]
    pl.semaphore_wait(barrier, n - 1)

    def gather(buffer, send, recv, low=0, count=None):
        def hop(block, device, number):
            held = buffer.at[block] if count is None else buffer.at[block, pl.ds(low, count)]
            return remote(held, held, send.at[number], recv.at[block], device)

        def begin():
            hop(me, y_peer, 0).start()
            for dz in range(1, NZ):
                hop(me, place(lax.rem(z + dz, NZ), y, core), dz).start()
            hop(me, c_peer, NZ).start()

        def middle():
            for dz in range(1, NZ):
                block = place(lax.rem(z + dz, NZ), y, core)
                hop(block, y_peer, 0).wait_recv()
                hop(block, y_peer, NZ + dz).start()
                hop(block, c_peer, 2 * NZ - 1 + dz).start()

        def late():
            for dz in range(NZ):
                block = place(lax.rem(z + dz, NZ), 1 - y, core)
                hop(block, c_peer, 0).wait_recv()
                hop(block, c_peer, 3 * NZ - 1 + dz).start()

        def finish():
            for dz in range(NZ):
                for py in range(NY):
                    hop(place(lax.rem(z + dz, NZ), py, 1 - core), c_peer, 0).wait_recv()

        def drain():
            for number in range(n - 1):
                hop(me, c_peer, number).wait_send()

        return begin, middle, late, finish, drain

    def exchange(source, target, send, recv, spread):
        def copy(to, slot, device):
            part_of = source.at[me] if spread else source.at[to]
            return remote(part_of, target.at[slot], send.at[to], recv.at[slot], device)

        def begin():
            def one(d, carry):
                to = lax.rem(me + d, n)
                copy(to, me, to).start()
                return carry

            lax.fori_loop(1, n, one, 0)

        def finish():
            def one(d, carry):
                other = lax.rem(me + d, n)
                copy(other, other, other).wait_recv()
                return carry

            lax.fori_loop(1, n, one, 0)

        def drain():
            def one(d, carry):
                other = lax.rem(me + d, n)
                copy(other, other, other).wait_send()
                return carry

            lax.fori_loop(1, n, one, 0)

        return begin, finish, drain

    cut = (groups + 1) // 2
    x_halves = [
        gather(xall, xs.at[0], xr.at[0], 0, cut),
        gather(xall, xs.at[1], xr.at[1], cut, groups + 1 - cut),
    ]
    b_gather = gather(ball, bs, br)
    low_scatter = exchange(lowp, lowr, l1s, l1r, False)
    low_spread = exchange(lowall, lowall, l2s, l2r, True)
    proj_swap = exchange(projs, projr, ps, pr, False)
    att_swap = exchange(atts, attr, ats, atr, False)
    lp_spread = exchange(lpall, lpall, gs, gr, True)

    for half in x_halves:
        half[0]()

    own_gained = (own * gain_row).astype(BF16)
    down = jnp.concatenate([aq_ref[...], ak_ref[...], av_ref[...], jnp.zeros((rank, part), BF16)], axis=0)
    low_part = dot_nt(own_gained, down)
    square = jnp.sum(own * own, axis=-1, keepdims=True)
    lane = lax.broadcasted_iota(jnp.int32, low_part.shape, 1)
    lowp[...] = jnp.where(lane < 3 * rank, low_part, square).reshape(lowp.shape)
    lowr[me] = lowp[me]
    low_scatter[0]()

    loads[8].wait()
    upm[...] = jnp.zeros_like(upm)
    upm[0:rank, 0:qcols] = bq_ref[...]
    empty = jnp.zeros(bk_ref.shape, F32)
    upm[rank : 2 * rank, qcols:] = jnp.concatenate([bk_ref[...].astype(F32), empty], axis=1).astype(BF16)
    upm[2 * rank : 3 * rank, qcols:] = jnp.concatenate([empty, bv_ref[...].astype(F32)], axis=1).astype(BF16)
    for r in range(2):
        keys[r, span:padded] = jnp.zeros((padded - span, keys.shape[2]), BF16)
        vals[r, span:padded] = jnp.zeros((padded - span, vals.shape[2]), BF16)
    sub8 = lax.broadcasted_iota(jnp.int32, (rows8, head), 0)
    lane8 = lax.broadcasted_iota(jnp.int32, (rows8, head), 1)
    position = jnp.where(sub8 < steps, len_ref[0] + sub8, len_ref[1] + sub8 - steps).astype(F32)
    angle = position * freq_ref[...]
    cosine = jnp.cos(angle)[None]
    sine = jnp.sin(angle)
    sine = jnp.where(lane8 < head // 2, -sine, sine)[None]

    sub_pick = lax.broadcasted_iota(jnp.int32, pick.shape, 0)
    row_pick = lax.broadcasted_iota(jnp.int32, pick.shape, 1) // steps
    chosen = jnp.zeros(pick.shape, F32)
    owned = jnp.int32(0)
    for row in range(row_count):
        mine = (owner_ref[row] == me).astype(jnp.int32)
        chosen = chosen + jnp.where((sub_pick == owned) & (row_pick == row), mine, 0).astype(F32)
        owned = owned + mine
    pick[...] = chosen

    for half in x_halves:
        half[1]()
    low_scatter[1]()
    lowall[me] = jnp.sum(lowr[...], axis=0)
    low_spread[0]()
    for half in x_halves:
        half[2]()
    for load in loads[:3]:
        load.wait()
    for half in x_halves:
        half[3]()
    b_gather[0]()

    pair = NC * part
    for m in range(n // 2):
        sides, kept = [], []
        for b in (2 * m, 2 * m + 1):
            block = xall[b, 0:groups].astype(F32).reshape(rows, part)
            sides.append(block * xall[b, groups].astype(F32)[0:1])
            kept.append(xall[b, me].astype(F32))
        gained = jnp.concatenate(sides, axis=1).astype(BF16)
        xres[:, m * pair : (m + 1) * pair] = jnp.concatenate(kept, axis=1)
        more_q = dot_nn(gained, wq[m * pair : (m + 1) * pair, :])
        more_kv = dot_nt(gained, wkv[:, m * pair : (m + 1) * pair])
        accq[...] = more_q if m == 0 else accq[...] + more_q
        acckv[...] = more_kv if m == 0 else acckv[...] + more_kv

    low_spread[1]()
    low_all = lowall[...].reshape(rows, lowall.shape[2])
    inverse = lax.rsqrt(low_all[:, 3 * rank : 3 * rank + 1] / width + EPSILON)
    low_high, low_low = split_high_low(jnp.where(lane < 3 * rank, low_all * inverse, 0.0))
    lifted = dot_nn(low_high, upm[...]) + dot_nn(low_low, upm[...])
    projs[:, :, 0:qcols] = (accq[...] * inverse + lifted[:, 0:qcols]).reshape(groups, rows8, qcols).astype(BF16)
    projs[:, :, qcols:] = (acckv[...] * inverse + lifted[:, qcols:]).reshape(groups, rows8, head).astype(BF16)
    projr[me] = projs[me]
    proj_swap[0]()
    proj_swap[1]()
    b_gather[1]()

    def normed_heads(values, gain_row):
        scaled = values * lax.rsqrt(jnp.mean(values * values, axis=-1, keepdims=True) + EPSILON)
        scaled = scaled * gain_row[...].astype(F32)[None]
        return scaled * cosine + pltpu.roll(scaled, head // 2, 2) * sine

    sub16 = lax.broadcasted_iota(jnp.int32, (n, rows8, head), 1)
    by_row = [[], []]
    for p in range(qcols // (2 * head)):
        first = normed_heads(projr[:, :, 2 * p * head : (2 * p + 1) * head].astype(F32), qg_ref)
        second = normed_heads(projr[:, :, (2 * p + 1) * head : (2 * p + 2) * head].astype(F32), qg_ref)
        by_row[0].append(jnp.where(sub16 < steps, first, pltpu.roll(second, steps, 1)))
        by_row[1].append(jnp.where(sub16 < steps, pltpu.roll(first, steps, 1), second))
    kv_groups = n // 2
    kv_all = projr[:, :, qcols:].astype(F32).reshape(kv_groups, 2, rows8, head)
    even, odd = kv_all[:, 0], kv_all[:, 1]
    lane_kv = lax.broadcasted_iota(jnp.int32, even.shape, 2)
    new_keys = normed_heads(jnp.where(lane_kv < head // 2, even, pltpu.roll(odd, head // 2, 2)), kg_ref)
    new_vals = jnp.where(lane_kv < head // 2, pltpu.roll(even, head // 2, 2), odd)

    for load in loads[3:7]:
        load.wait()
    blank = jnp.zeros((rows8, head), F32)
    for g in range(kv_groups):
        new_key = jnp.concatenate([new_keys[g], blank], axis=0).astype(BF16)
        new_val = jnp.concatenate([new_vals[g], blank], axis=0).astype(BF16)
        for r in range(2):
            keys[r, span : span + 2 * rows8, g * head : (g + 1) * head] = new_key
            vals[r, span : span + 2 * rows8, g * head : (g + 1) * head] = new_val

    asked = 4 * rows8
    column = lax.broadcasted_iota(jnp.int32, (asked, padded), 1)
    step_of = lax.rem(lax.broadcasted_iota(jnp.int32, (asked, padded), 0), steps)
    live = []
    for r in range(2):
        fresh = column - span - r * steps
        in_cache = (column < len_ref[r]) & (column < span)
        live.append((in_cache | ((fresh >= 0) & (fresh <= step_of) & (column >= span))).astype(F32))
    sub4 = lax.broadcasted_iota(jnp.int32, (4, rows8, head), 1)
    for g in range(kv_groups):
        outs = []
        for r in range(2):
            tiles = [by_row[r][p][2 * g + side][None] for side in range(2) for p in range(2)]
            query = jnp.concatenate(tiles, axis=0).reshape(asked, head).astype(BF16)
            scores = dot_nt(query, keys[r, :, g * head : (g + 1) * head]) * (1.0 / math.sqrt(head))
            weights = jnp.exp(scores) * live[r]
            total = jnp.sum(weights, axis=-1, keepdims=True)
            mixed = dot_nn(weights.astype(BF16), vals[r, :, g * head : (g + 1) * head]) / total
            outs.append(mixed.reshape(4, rows8, head))
        first = jnp.where(sub4 < steps, outs[0], pltpu.roll(outs[1], steps, 1)).astype(BF16)
        second = jnp.where(sub4 < steps, pltpu.roll(outs[0], steps, 1), outs[1]).astype(BF16)
        for side in range(2):
            for p in range(2):
                atts[2 * g + side, :, 2 * p * head : (2 * p + 1) * head] = first[2 * side + p]
                atts[2 * g + side, :, (2 * p + 1) * head : (2 * p + 2) * head] = second[2 * side + p]
    attr[me] = atts[me]
    att_swap[0]()
    b_gather[2]()
    b_gather[3]()
    for m in range(n // 2):
        bfull[:, m * pair : (m + 1) * pair] = jnp.concatenate(
            [ball[2 * m].astype(F32), ball[2 * m + 1].astype(F32)], axis=1
        ).astype(BF16)
    for load in (loads[7], loads[9], loads[10]):
        load.wait()
    att_swap[1]()

    segment = attr[...].astype(F32).reshape(rows, qcols).astype(BF16)
    inner_high, inner_low = split_high_low(dot_nt(segment, ao_ref[...]))

    def c_hop(k):
        return remote(parts.at[k, 1 - core], got_c.at[k], cs.at[k], cr.at[k], c_peer)

    def y_hop(k):
        return remote(half_y.at[k, 1 - y], got_y.at[k], ys.at[k], yr.at[k], y_peer)

    def z_hop(k, dz):
        other = lax.rem(z + dz, NZ)
        return remote(quarter.at[k, other], got_z.at[k, dz - 1], zs.at[k, dz - 1], zr.at[k, dz - 1], place(other, y, core))

    def multiply(k):
        at = slice(k * chunk, (k + 1) * chunk)
        up = bfull[:, at]
        out = dot_nn(segment, wo[:, at]) + (dot_nn(inner_high, up) + dot_nn(inner_low, up))
        out = out.reshape(groups // NC, NC, rows8, chunk).astype(BF16)
        for pc in range(NC):
            parts[k, pc] = out[:, pc]
        c_hop(k).start()

    def over_y(k):
        c_hop(k).wait_recv()
        both = parts[k, core].astype(F32) + got_c[k].astype(F32)
        both = both.reshape(NZ, NY, rows8, chunk).astype(BF16)
        for py in range(NY):
            half_y[k, py] = both[:, py]
        y_hop(k).start()

    def over_z(k):
        y_hop(k).wait_recv()
        quarter[k] = (half_y[k, y].astype(F32) + got_y[k].astype(F32)).astype(BF16)
        for dz in range(1, NZ):
            z_hop(k, dz).start()

    for k in range(CHUNKS):
        multiply(k)
        if k >= 1:
            over_y(k - 1)
    over_y(CHUNKS - 1)
    for k in range(CHUNKS):
        over_z(k)

    squares = jnp.zeros((rows8, 1), F32)
    for k in range(CHUNKS):
        at = slice(k * chunk, (k + 1) * chunk)
        total = xres[:, at] + quarter[k, z].astype(F32)
        for dz in range(1, NZ):
            z_hop(k, dz).wait_recv()
            total = total + got_z[k, dz - 1].astype(F32)
        rounded = total.astype(BF16)
        rounded = rounded.astype(F32)
        for row in range(2):
            hid_ref[row, :, at] = rounded[row * steps : (row + 1) * steps].astype(BF16)
        hidden[:, at] = rounded
        squares = squares + jnp.sum(rounded * rounded, axis=-1, keepdims=True)
    final = (hidden[...] * lax.rsqrt(squares / width + EPSILON) * fg_ref[...].astype(F32)[None, :]).astype(BF16)
    cands = cand_ref.shape[1]
    logits = jnp.where(
        lax.broadcasted_iota(jnp.int32, (rows8, cands), 0) < steps,
        dot_nt(final, cand_ref[0]),
        dot_nt(final, cand_ref[1]),
    )
    logprob = logits - jnp.log(jnp.sum(jnp.exp(logits), axis=-1, keepdims=True))
    spaced = jnp.concatenate(
        [logprob] * steps + [jnp.zeros((rows8, lpall.shape[2] - steps * cands), F32)], axis=1
    )
    lane_lp = lax.broadcasted_iota(jnp.int32, spaced.shape, 1)
    step_lp = lax.rem(lax.broadcasted_iota(jnp.int32, spaced.shape, 0), steps)
    lpall[me] = jnp.where(lane_lp // cands == step_lp, spaced, 0.0)
    lp_spread[0]()
    lp_spread[1]()
    placed = jnp.dot(
        pick[...], lpall[...].reshape(rows, lpall.shape[2]),
        precision=lax.Precision.HIGHEST, preferred_element_type=F32,
    )
    lp_ref[...] = placed[0 : lp_ref.shape[0], 0 : lp_ref.shape[1]]

    for half in x_halves:
        half[4]()
    b_gather[4]()
    for swap in (low_scatter, low_spread, proj_swap, att_swap, lp_spread):
        swap[2]()
    for k in range(CHUNKS):
        c_hop(k).wait_send()
        y_hop(k).wait_send()
        for dz in range(1, NZ):
            z_hop(k, dz).wait_send()


def fused_on_device(
    x_in, ln_gain, w_query, w_key, w_value, w_out, q_gain, k_gain, a_query, a_key, a_value,
    b_query, b_key, b_value, a_out, b_out, key_cache, value_cache, kv_length, cand_rows,
    final_gain, row_owner,
):
    n = lax.axis_size("tp")
    me = lax.axis_index("tp")
    row_count, step_count, part = x_in.shape
    rows8 = row_count * step_count // n
    width = part * n
    head = q_gain.shape[0]
    qcols = w_query.shape[1]
    kvcols = w_key.shape[1]
    cols = qcols + 2 * kvcols
    rank = a_query.shape[1]
    span, kv_width = key_cache.shape[1:]
    cands = cand_rows.shape[1]
    half = head // 2
    frequency = ROPE_BASE ** (-np.arange(half, dtype=np.float32) / np.float32(half))
    frequency = jnp.asarray(np.concatenate([frequency, frequency])[None, :].astype(np.float32))

    chunk = width // CHUNKS
    rows = row_count * step_count
    padded = span + 128
    vmem = pl.BlockSpec(memory_space=pltpu.VMEM)
    smem = pl.BlockSpec(memory_space=pltpu.SMEM)
    hbm = pl.BlockSpec(memory_space=pl.ANY)
    dma = pltpu.SemaphoreType.DMA
    return pl.pallas_call(
        fused_kernel,
        out_shape=(
            jax.ShapeDtypeStruct((row_count // n, step_count, width), BF16),
            jax.ShapeDtypeStruct((CAP, step_count * cands), F32),
        ),
        in_specs=[vmem, vmem, hbm, hbm, hbm, hbm, vmem, vmem, vmem, vmem, vmem,
                  hbm, vmem, vmem, hbm, vmem, hbm, hbm, smem, hbm, vmem, vmem, smem],
        out_specs=(vmem, vmem),
        scratch_shapes=[
            pltpu.VMEM((width, qcols), BF16),
            pltpu.VMEM((2 * kvcols, width), BF16),
            pltpu.VMEM((qcols, width), BF16),
            pltpu.VMEM((2, padded, kv_width), BF16),
            pltpu.VMEM((2, padded, kv_width), BF16),
            pltpu.VMEM((n, n + 1, rows8, part), BF16),
            pltpu.VMEM((n, rank, part), BF16),
            pltpu.VMEM((n, rows8, 4 * rank), F32),
            pltpu.VMEM((n, rows8, 4 * rank), F32),
            pltpu.VMEM((n, rows8, 4 * rank), F32),
            pltpu.VMEM((4 * rank, cols), BF16),
            pltpu.VMEM((rows, qcols), F32),
            pltpu.VMEM((rows, 2 * kvcols), F32),
            pltpu.VMEM((rows8, width), F32),
            pltpu.VMEM((rank, width), BF16),
            pltpu.VMEM(b_query.shape, BF16),
            pltpu.VMEM((rank, qcols), BF16),
            pltpu.VMEM(cand_rows.shape, BF16),
            pltpu.VMEM((8, rows), F32),
            pltpu.VMEM((n, rows8, cols), BF16),
            pltpu.VMEM((n, rows8, cols), BF16),
            pltpu.VMEM((n, rows8, qcols), BF16),
            pltpu.VMEM((n, rows8, qcols), BF16),
            pltpu.VMEM((CHUNKS, NC, NZ * NY, rows8, chunk), BF16),
            pltpu.VMEM((CHUNKS, NZ * NY, rows8, chunk), BF16),
            pltpu.VMEM((CHUNKS, NY, NZ, rows8, chunk), BF16),
            pltpu.VMEM((CHUNKS, NZ, rows8, chunk), BF16),
            pltpu.VMEM((CHUNKS, NZ, rows8, chunk), BF16),
            pltpu.VMEM((CHUNKS, NZ - 1, rows8, chunk), BF16),
            pltpu.VMEM((rows8, width), F32),
            pltpu.VMEM((n, rows8, 128), F32),
            dma((11,)),
            dma((2, n)), dma((2, n)), dma((n,)), dma((n,)),
            dma((n,)), dma((n,)), dma((n,)), dma((n,)),
            dma((n,)), dma((n,)), dma((n,)), dma((n,)),
            dma((CHUNKS,)), dma((CHUNKS,)), dma((CHUNKS,)), dma((CHUNKS,)),
            dma((CHUNKS, NZ - 1)), dma((CHUNKS, NZ - 1)),
            dma((n,)), dma((n,)),
        ],
        compiler_params=pltpu.CompilerParams(
            collective_id=0, has_side_effects=True, vmem_limit_bytes=56 * 1024 * 1024
        ),
        name="layer",
    )(
        x_in, ln_gain, w_query, w_key.T, w_value.T, w_out,
        q_gain[None, :], k_gain[None, :], a_query.T, a_key.T, a_value.T, b_query, b_key, b_value,
        a_out.T, b_out, key_cache, value_cache, kv_length, cand_rows, final_gain,
        frequency, row_owner[:, 0],
    )


def solution(mesh):
    placed = (
        P("parts", None, "tp"),
        P("tp"),
        P(None, "tp"),
        P(None, "tp"),
        P(None, "tp"),
        P("tp", None),
        P(),
        P(),
        P("tp", None),
        P("tp", None),
        P("tp", None),
        P(None, "tp"),
        P(None, "tp"),
        P(None, "tp"),
        P("tp", None),
        P(None, "tp"),
        P(("parts", "tp"), None, None),
        P(("parts", "tp"), None, None),
        P(("parts", "tp")),
        P(("parts", "tp"), None, None),
        P(),
        P("parts", None),
    )
    return jax.shard_map(
        fused_on_device if mesh.shape["tp"] == FUSED_TP else on_device,
        mesh=mesh,
        in_specs=placed,
        out_specs=(P(("parts", "tp"), None, None), P(("parts", "tp"), None)),
        check_vma=False,
    )
```
